32 devices in a mesh: morton: 8 (over z, y), sub: 4 (over x, core).
Axes of the slice: x: 2, y: 2, z: 4, core: 2. Of those that a mesh axis runs over, the one named last changes fastest.
Arguments:
- multipoles: bfloat16 [2048, 128], P(('morton', 'sub')), may hold values from -6 to 6
- translations: bfloat16 [316, 128, 128], P('sub'), may hold values from -0.0625 to 0.0625
- upward_ops: bfloat16 [8, 128, 128], replicated, may hold values from -0.1875 to 0.1875
- downward_ops: bfloat16 [8, 128, 128], replicated, may hold values from -0.375 to 0.375
- targets_l6: int32 [8, 316, 128], P('morton', 'sub'), may hold values from 0 to 255, as said below
- source_boxes_level6: int32 [8, 316, 128], P('morton', 'sub'), may hold values from 0 to 767, as said below
- counts_l6: int32 [8, 316], P('morton', 'sub'), may hold values from 1 to 128, as said below
- target_boxes_level5: int32 [8, 316, 16], P('morton', 'sub'), may hold values from 0 to 31, as said below
- anchors_l5: int32 [8, 316, 16], P('morton', 'sub'), may hold values from 0 to 255, as said below
- counts_l5: int32 [8, 316], P('morton', 'sub'), may hold values from 1 to 16, as said below
- targets_l4: int32 [8, 316, 2], P('morton', 'sub'), may hold values from 0 to 3, as said below
- anchors_l4: int32 [8, 316, 2], P('morton', 'sub'), may hold values from 0 to 31, as said below
- counts_l4: int32 [8, 316], P('morton', 'sub'), may hold values from 1 to 2, as said below
Outputs:
- local_exp: bfloat16 [2048, 128], P(('morton', 'sub'))
The draws below stay inside these ranges and needn't reach their ends.
Inputs may be any that keep to these rules, and one draw needn't show every extreme that they name: `targets_l6`: targets of one operator's block within one subtree are its level-6 boxes. `source_boxes_level6`: sources lie in the previous, own or next subtree, at most 256 boxes before or after the target. `counts_l6`: some block of every subtree is full. `target_boxes_level5`: targets are level-5 boxes of the subtree. `anchors_l5`: sources are level-5 boxes of the aligned group of 8 subtrees. `counts_l5`: some block of every subtree is full. `targets_l4`: targets are level-4 boxes of the subtree. `anchors_l4`: sources are level-4 boxes of the aligned group of 8 subtrees. `counts_l4`: some block of every subtree is full.
All inputs are finite; a program needn't handle non-finite values.
Results may differ from the reference program's by a relative error of at most 0.011.
Values may be sent and summed in bfloat16 or wider, within the bound.
A program may use at most 64 MiB of HBM per device.

```python
import jax
import jax.numpy as jnp
from jax import lax

R = 128
NOPS = 316
B6M = 256
SUBTREES = 8
B5M = 32
B4M = 4
CAP6 = 128
CAP5 = 16
CAP4 = 2
NB6 = 2048
N_SUB = 4


def pair_tables(key, box_count, capacity, level_tag, halo_space):
    key = jax.random.fold_in(key, level_tag)
    key_list = jax.random.split(key, 6)
    table_shape = (SUBTREES, NOPS, capacity)
    chosen = jax.random.randint(key_list[4], (SUBTREES, 1), 0, NOPS)
    is_chosen = jnp.arange(NOPS, dtype=jnp.int32)[None, :] == chosen
    chosen_block = is_chosen[:, :, None]
    begins = jax.random.randint(key_list[0], (SUBTREES, NOPS, 1), 0, box_count)
    begins = jnp.where(chosen_block, box_count - 1, begins)
    strides = 2 * jax.random.randint(key_list[1], (SUBTREES, NOPS, 1), 0, max(box_count // 2, 1)) + 1
    strides = jnp.where(chosen_block, 1, strides)
    slot_numbers = jnp.arange(capacity, dtype=jnp.int32)[None, None, :]
    targets = (begins + strides * slot_numbers) % box_count
    leading_slot = jnp.logical_and(chosen_block, slot_numbers == 0)
    second_slot = jnp.logical_and(chosen_block, slot_numbers == 1)
    if halo_space:
        offsets = jax.random.randint(key_list[2], table_shape, 0, 2 * box_count + 1)
        offsets = jnp.where(leading_slot, 2 * box_count, jnp.where(second_slot, 0, offsets))
        anchors = targets + offsets
    else:
        anchors = jax.random.randint(key_list[2], table_shape, 0, 8 * box_count)
        anchors = jnp.where(leading_slot, 8 * box_count - 1, jnp.where(second_slot, 0, anchors))
    filled = jax.random.randint(key_list[3], (SUBTREES, NOPS), 0, 7) == 0
    filled = jnp.logical_or(filled, is_chosen)
    counts = jnp.where(filled, capacity, jax.random.randint(key_list[5], (SUBTREES, NOPS), 1, capacity + 1))
    return (targets.astype(jnp.int32), anchors.astype(jnp.int32), counts.astype(jnp.int32))


def draw_targets_l6(key, part):
    return pair_tables(key, B6M, CAP6, 6, True)[0]


def draw_source_boxes_level6(key, part):
    return pair_tables(key, B6M, CAP6, 6, True)[1]


def draw_counts_l6(key, part):
    return pair_tables(key, B6M, CAP6, 6, True)[2]


def draw_target_boxes_level5(key, part):
    return pair_tables(key, B5M, CAP5, 5, False)[0]


def draw_anchors_l5(key, part):
    return pair_tables(key, B5M, CAP5, 5, False)[1]


def draw_counts_l5(key, part):
    return pair_tables(key, B5M, CAP5, 5, False)[2]


def draw_targets_l4(key, part):
    return pair_tables(key, B4M, CAP4, 4, False)[0]


def draw_anchors_l4(key, part):
    return pair_tables(key, B4M, CAP4, 4, False)[1]


def draw_counts_l4(key, part):
    return pair_tables(key, B4M, CAP4, 4, False)[2]


def block_levels(key, shape, shards, least, largest):
    def one(dim, blocks):
        steps = jax.random.uniform(jax.random.fold_in(jax.random.fold_in(key, 6), dim), (blocks,), jnp.float32, least / len(shards), largest / len(shards))
        return jnp.repeat(jnp.exp(steps), shape[dim] // blocks).reshape((-1,) + (1,) * (len(shape) - dim - 1))

    factor_of = one(*shards[0])
    for cut in shards[1:]:
        factor_of = factor_of * one(*cut)
    return factor_of


def centred(rng, extent, scale, limit, cuts=(), kind=jnp.bfloat16):
    loudness = block_levels(rng, extent, cuts, -0.22, 0.18) if cuts else 1.0
    entries = jax.random.normal(rng, extent, jnp.float32) * scale * loudness
    return jnp.minimum(jnp.maximum(entries, -limit), limit).astype(kind)


def setup_inputs(seed: int = 0) -> dict:
    seeds = jax.random.split(jax.random.key(seed), 14)
    multipoles = centred(seeds[0], (NB6, R), 1.0, 6.0, ((0, 32),))
    translations = centred(seeds[1], (NOPS, R, R), (64 * R) ** -0.5, 0.0625, ((0, 4),))
    upward_ops = centred(seeds[2], (8, R, R), (8 * R) ** -0.5, 0.1875)
    downward_ops = centred(seeds[3], (8, R, R), (2 * R) ** -0.5, 0.375)
    targets_l6 = draw_targets_l6(jax.random.fold_in(seeds[13], 71), 0)
    source_boxes_level6 = draw_source_boxes_level6(jax.random.fold_in(seeds[13], 71), 0)
    counts_l6 = draw_counts_l6(jax.random.fold_in(seeds[13], 71), 0)
    target_boxes_level5 = draw_target_boxes_level5(jax.random.fold_in(seeds[13], 71), 0)
    anchors_l5 = draw_anchors_l5(jax.random.fold_in(seeds[13], 71), 0)
    counts_l5 = draw_counts_l5(jax.random.fold_in(seeds[13], 71), 0)
    targets_l4 = draw_targets_l4(jax.random.fold_in(seeds[13], 71), 0)
    anchors_l4 = draw_anchors_l4(jax.random.fold_in(seeds[13], 71), 0)
    counts_l4 = draw_counts_l4(jax.random.fold_in(seeds[13], 71), 0)
    return dict(multipoles=multipoles, translations=translations, upward_ops=upward_ops, downward_ops=downward_ops, targets_l6=targets_l6, source_boxes_level6=source_boxes_level6, counts_l6=counts_l6, target_boxes_level5=target_boxes_level5, anchors_l5=anchors_l5, counts_l5=counts_l5, targets_l4=targets_l4, anchors_l4=anchors_l4, counts_l4=counts_l4)


def translate_block(expansions, targets, anchors, counts, kernels, row_count, factor):
    operator_matrices, capacity = targets.shape
    coeff_width = expansions.shape[1]
    block_rows = min(capacity, 128)
    turn_count = capacity // block_rows
    target_steps = targets.reshape(operator_matrices, turn_count, block_rows).transpose(1, 0, 2)
    anchor_steps = anchors.reshape(operator_matrices, turn_count, block_rows).transpose(1, 0, 2)
    slot_steps = jnp.arange(capacity, dtype=jnp.int32).reshape(turn_count, block_rows)
    wide_kernels = kernels.astype(jnp.float32)

    def single_rotation(totals, inputs):
        target_rows, anchor_rows, slot_numbers = inputs
        picked = expansions[anchor_rows].astype(jnp.float32)
        product = jnp.einsum("obr,ors->obs", picked, wide_kernels, precision=lax.Precision.HIGHEST)
        is_live = slot_numbers[None, :] < counts[:, None]
        product = jnp.where(is_live[:, :, None], product, 0.0) * factor
        return totals.at[target_rows.reshape(-1)].add(product.reshape(-1, coeff_width)), None

    totals, _ = lax.scan(single_rotation, jnp.zeros((row_count, coeff_width), jnp.float32), (target_steps, anchor_steps, slot_steps))
    return totals


def upward(children, operator_matrices):
    parents = children.shape[0] // 8
    grouped_rows = children.reshape(parents, 8, children.shape[1]).astype(jnp.float32)
    summed_values = jnp.einsum("duo,uob->db", grouped_rows, operator_matrices.astype(jnp.float32), precision=lax.Precision.HIGHEST)
    return summed_values.astype(jnp.bfloat16)


def downward(parent, operator_matrices):
    spread = jnp.einsum("pr,crs->pcs", parent.astype(jnp.float32), operator_matrices.astype(jnp.float32), precision=lax.Precision.HIGHEST)
    return spread.reshape(-1, parent.shape[1])


def reference(multipoles, translations, upward_ops, downward_ops, targets_l6, source_boxes_level6, counts_l6, target_boxes_level5, anchors_l5, counts_l5, targets_l4, anchors_l4, counts_l4):
    coeff_width = multipoles.shape[1]
    blank = jnp.zeros((B6M, coeff_width), jnp.bfloat16)
    padded = jnp.concatenate([blank, multipoles, blank], axis=0)
    coarse5 = upward(multipoles, upward_ops)
    coarse4 = upward(coarse5, upward_ops)
    subtree_ids = jnp.arange(SUBTREES, dtype=jnp.int32)
    group_size = NOPS // N_SUB

    def level_six(subtree):
        nearby = lax.dynamic_slice_in_dim(padded, subtree * B6M, 3 * B6M, 0)
        total = jnp.zeros((B6M, coeff_width), jnp.float32)
        for group in range(N_SUB):
            first = group * group_size
            last = first + group_size
            partial_value = translate_block(nearby, targets_l6[subtree, first:last], source_boxes_level6[subtree, first:last], counts_l6[subtree, first:last], translations[first:last], B6M, 1.0)
            rounded = lax.optimization_barrier(partial_value.astype(jnp.bfloat16))
            total = total + rounded.astype(jnp.float32)
        return total

    def level_five(subtree):
        group_rows = lax.dynamic_slice_in_dim(coarse5, (subtree // 8) * (8 * B5M), 8 * B5M, 0)
        return translate_block(group_rows, target_boxes_level5[subtree], anchors_l5[subtree], counts_l5[subtree], translations, B5M, 0.5)

    def level_four(subtree):
        group_rows = lax.dynamic_slice_in_dim(coarse4, (subtree // 8) * (8 * B4M), 8 * B4M, 0)
        return translate_block(group_rows, targets_l4[subtree], anchors_l4[subtree], counts_l4[subtree], translations, B4M, 0.25)

    far_six = lax.map(level_six, subtree_ids).reshape(-1, coeff_width)
    far_five = lax.map(level_five, subtree_ids).reshape(-1, coeff_width)
    far_four = lax.map(level_four, subtree_ids).reshape(-1, coeff_width)
    local4 = far_four.astype(jnp.bfloat16)
    local5 = (far_five + downward(local4, downward_ops)).astype(jnp.bfloat16)
    return (far_six + downward(local5, downward_ops)).astype(jnp.bfloat16)
```

```python
import functools

import jax
import jax.numpy as jnp
from jax import lax
from jax.experimental import pallas as pl
from jax.experimental.pallas import tpu as pltpu
from jax.sharding import PartitionSpec as P

BF16 = jnp.bfloat16
F32 = jnp.float32
MESH = pl.DeviceIdType.MESH
GROUP = 8
PACK = 16
STEP = 16


def dot(a, b):
    return jnp.dot(a, b, preferred_element_type=F32)


def dot_nt(a, b):
    return lax.dot_general(a, b, (((1,), (1,)), ((), ())), preferred_element_type=F32)


def upward_into(mult_ref, up_ref, wide, pack):
    parents = mult_ref.shape[0] // 8
    wide[...] = mult_ref[...].astype(F32)
    children = [wide[pl.ds(c, parents, stride=8), :] for c in range(8)]
    lhs = jnp.concatenate(children, axis=1).astype(BF16)
    ops = up_ref[...].reshape(-1, up_ref.shape[2])
    five = dot(lhs, ops).astype(BF16).astype(F32)
    row = jnp.concatenate([five[c : c + 1, :] for c in range(8)], axis=1).astype(BF16)
    four = dot(row, ops)
    pad = jnp.zeros((PACK - parents - 1, five.shape[1]), F32)
    pack[...] = jnp.concatenate([five, four, pad], axis=0).astype(BF16)


def peers_of(sizes):
    n_m, n_s = sizes
    m, s = lax.axis_index("morton"), lax.axis_index("sub")
    base = m // GROUP * GROUP
    mine = (m - base) * n_s + s

    def group_peer(k):
        slot = (mine + k) % (GROUP * n_s)
        return slot, (base + slot // n_s, slot % n_s)

    def halo_peer(k):
        shift = k // n_s * 2 - 1
        return shift, ((m + shift + n_m) % n_m, k % n_s)

    return m, s, mine, group_peer, halo_peer


def exchange_kernel(
    sizes, mult_ref, up_ref, near_ref, coarse_ref, wide, pack,
    near_send, near_recv, coarse_send, coarse_recv,
):
    n_m, n_s = sizes
    m, s, mine, group_peer, halo_peer = peers_of(sizes)
    slots = GROUP * n_s
    upward_into(mult_ref, up_ref, wide, pack)

    barrier = pltpu.get_barrier_semaphore()

    def greet(k, _):
        pl.semaphore_signal(barrier, inc=1, device_id=group_peer(k)[1], device_id_type=MESH)
        return 0

    def greet_halo(k, _):
        pl.semaphore_signal(barrier, inc=1, device_id=halo_peer(k)[1], device_id_type=MESH)
        return 0

    lax.fori_loop(1, slots, greet, 0)
    expected = slots - 1
    if n_m > GROUP:
        lax.fori_loop(0, 2 * n_s, greet_halo, 0)
        expected = expected + 2 * n_s
    pl.semaphore_wait(barrier, expected)

    def coarse_copy(k, there):
        slot, peer = group_peer(k)
        return pltpu.make_async_remote_copy(
            src_ref=pack,
            dst_ref=coarse_ref.at[slot if there else mine],
            send_sem=coarse_send.at[k],
            recv_sem=coarse_recv.at[slot if there else mine],
            device_id=peer,
            device_id_type=MESH,
        )

    def sub_copy(k, there):
        other = (s + k) % n_s
        lands = n_s + (other if there else s)
        return pltpu.make_async_remote_copy(
            src_ref=mult_ref,
            dst_ref=near_ref.at[lands],
            send_sem=near_send.at[2 * n_s + k],
            recv_sem=near_recv.at[lands],
            device_id=(m, other),
            device_id_type=MESH,
        )

    def halo_copy(k, there):
        shift, peer = halo_peer(k)
        lands = (1 + shift) * n_s + peer[1] if there else (1 - shift) * n_s + s
        return pltpu.make_async_remote_copy(
            src_ref=mult_ref,
            dst_ref=near_ref.at[lands],
            send_sem=near_send.at[k],
            recv_sem=near_recv.at[lands],
            device_id=peer,
            device_id_type=MESH,
        )

    def each(first, last, act):
        def body(k, _):
            act(k)
            return 0

        lax.fori_loop(first, last, body, 0)

    each(0, 2 * n_s, lambda k: halo_copy(k, False).start())
    each(1, n_s, lambda k: sub_copy(k, False).start())
    each(1, slots, lambda k: coarse_copy(k, False).start())
    near_ref[n_s + s] = mult_ref[...]
    coarse_ref[mine] = pack[...]
    each(0, 2 * n_s, lambda k: halo_copy(k, True).wait_recv())
    each(1, n_s, lambda k: sub_copy(k, True).wait_recv())
    each(1, slots, lambda k: coarse_copy(k, True).wait_recv())
    each(0, 2 * n_s, lambda k: halo_copy(k, False).wait_send())
    each(1, n_s, lambda k: sub_copy(k, False).wait_send())
    each(1, slots, lambda k: coarse_copy(k, False).wait_send())


def one_hot(rows, height):
    ids = lax.broadcasted_iota(jnp.int32, (height, rows.shape[1]), 0).astype(F32)
    return jnp.where(ids == rows, 1.0, 0.0).astype(BF16)


def column_of(row, height):
    width = row.shape[1]
    at = lax.broadcasted_iota(jnp.int32, (height, width), 0)
    on = lax.broadcasted_iota(jnp.int32, (height, width), 1)
    return jnp.sum(jnp.where(at == on, row, 0.0), axis=1, keepdims=True)


def folded(values, per_row):
    n, cap = values.shape
    lanes = per_row * cap
    j = lax.broadcasted_iota(jnp.int32, (cap, lanes), 0)
    lane = lax.broadcasted_iota(jnp.int32, (cap, lanes), 1)
    spread = jnp.where(lane % cap == j, 1.0, 0.0).astype(BF16)
    wide = dot(values.astype(BF16), spread)
    at = lax.broadcasted_iota(jnp.int32, (n, lanes), 0)
    on = lax.broadcasted_iota(jnp.int32, (n, lanes), 1)
    wide = jnp.where(at % per_row == on // cap, wide, 0.0).astype(BF16)
    out = lax.broadcasted_iota(jnp.int32, (n // per_row, n), 0)
    src = lax.broadcasted_iota(jnp.int32, (n // per_row, n), 1)
    return dot(jnp.where(src // per_row == out, 1.0, 0.0).astype(BF16), wide)


def translate_kernel(
    n_m, near_ref, coarse_ref, tr_ref, t6_ref, s6_ref, c6_ref, t5_ref, s5_ref, c5_ref,
    t4_ref, s4_ref, c4_ref, out_ref, mats, mt, c5t, c4t, tg6, sr6, bl6, tg5, sr5, tg4, sr4,
    gather, total, sem,
):
    n_ops, width = tr_ref.shape[0], tr_ref.shape[2]
    padded = mats.shape[0]
    boxes = near_ref.shape[0] * near_ref.shape[1] // 3
    fives, fours = boxes // 8, boxes // 64
    cap6, cap5, cap4 = t6_ref.shape[2], t5_ref.shape[2], t4_ref.shape[2]
    copy = pltpu.make_async_copy(tr_ref, mats.at[pl.ds(0, n_ops)], sem)
    copy.start()
    for o in range(n_ops, padded):
        mats[o] = jnp.zeros(mats.shape[1:], BF16)

    m = lax.axis_index("morton")
    r = lax.broadcasted_iota(jnp.int32, (width, width), 0)
    c = lax.broadcasted_iota(jnp.int32, (width, width), 1)
    eye = jnp.where(r == c, 1.0, 0.0).astype(BF16)
    near = near_ref[...].reshape(3, boxes, width)
    for block in range(3):
        rows = dot_nt(eye, near[block])
        if block == 0:
            rows = jnp.where(m == 0, 0.0, rows)
        if block == 2:
            rows = jnp.where(m == n_m - 1, 0.0, rows)
        mt[pl.ds(block * width, width), :] = rows.astype(BF16)
    slots = coarse_ref.shape[0]
    packed = dot_nt(eye, coarse_ref[...].reshape(slots * PACK, width)).astype(BF16)
    q = lax.broadcasted_iota(jnp.int32, (slots * PACK, slots * 8), 0)
    p = lax.broadcasted_iota(jnp.int32, (slots * PACK, slots * 8), 1)
    c5t[...] = dot(packed, jnp.where(q == p // 8 * PACK + p % 8, 1.0, 0.0).astype(BF16)).astype(BF16)
    q = lax.broadcasted_iota(jnp.int32, (slots * PACK, slots), 0)
    p = lax.broadcasted_iota(jnp.int32, (slots * PACK, slots), 1)
    c4t[...] = dot(packed, jnp.where(q == p * PACK + 8, 1.0, 0.0).astype(BF16)).astype(BF16)

    def table(t_ref, c_ref, shift):
        cap = t_ref.shape[2]
        live = lax.broadcasted_iota(jnp.int32, (n_ops, cap), 1).astype(F32)
        live = live < column_of(c_ref[...].astype(F32), n_ops)
        return jnp.where(live, t_ref[0].astype(F32) + shift, shift - 1.0)

    def filled(values, fill):
        if padded == n_ops:
            return values
        more = jnp.full((padded - n_ops, values.shape[1]), fill, F32)
        return jnp.concatenate([values, more], axis=0)

    tg6[...] = filled(table(t6_ref, c6_ref, 0.0), -1.0)
    source = s6_ref[0]
    block = jnp.where(source >= boxes, 1, 0) + jnp.where(source >= 2 * boxes, 1, 0)
    sr6[...] = filled((source - block * boxes).astype(F32), 0.0)
    bl6[...] = filled(block.astype(F32), 0.0)

    def keys(t_ref, c_ref, per_row, height):
        raw = folded(filled(table(t_ref, c_ref, 1.0), 0.0), per_row)
        lane = lax.broadcasted_iota(jnp.int32, raw.shape, 1) // t_ref.shape[2]
        return jnp.where(raw > 0.0, raw - 1.0 + (lane * height).astype(F32), -1.0)

    tg5[...] = keys(t5_ref, c5_ref, 8, fives)
    sr5[...] = folded(filled(s5_ref[0].astype(F32), 0.0), 8)
    tg4[...] = keys(t4_ref, c4_ref, STEP, PACK)
    sr4[...] = folded(filled(s4_ref[0].astype(F32), 0.0), STEP)
    copy.wait()

    total[...] = jnp.zeros(total.shape, F32)
    zero = jnp.zeros((width, cap6), BF16)

    @pl.loop(0, padded // STEP)
    def _(step):
        for pair in range(STEP // 2):
            heads, places, picks = [], [], []
            for half in range(2):
                o = step * STEP + 2 * pair + half
                picks.append(one_hot(sr6[pl.ds(o, 1), :], boxes))
                places.append(one_hot(tg6[pl.ds(o, 1), :], boxes))
                heads.append(bl6[pl.ds(o, 1), :])
            found = dot(mt[...], jnp.concatenate(picks, axis=1))
            head = jnp.concatenate(heads, axis=1)
            found = jnp.where(
                head == 0.0,
                found[:width],
                jnp.where(head == 1.0, found[width : 2 * width], found[2 * width :]),
            ).astype(BF16)
            apart = jnp.concatenate(
                [
                    jnp.concatenate([found[:, :cap6], zero], axis=1),
                    jnp.concatenate([zero, found[:, cap6:]], axis=1),
                ],
                axis=0,
            )
            placed = dot_nt(jnp.concatenate(places, axis=1), apart)
            gather[pl.ds(0, boxes), pl.ds(pair * 2 * width, 2 * width)] = placed.astype(BF16)
        for half in range(STEP // 8):
            row = step * (STEP // 8) + half
            found = dot(c5t[...], one_hot(sr5[pl.ds(row, 1), :], c5t.shape[1])).astype(BF16)
            placed = dot_nt(one_hot(tg5[pl.ds(row, 1), :], 8 * fives), found).astype(BF16)
            for o in range(8):
                gather[pl.ds(boxes, fives), pl.ds((half * 8 + o) * width, width)] = placed[
                    o * fives : (o + 1) * fives
                ]
        found = dot(c4t[...], one_hot(sr4[pl.ds(step, 1), :], c4t.shape[1])).astype(BF16)
        placed = dot_nt(one_hot(tg4[pl.ds(step, 1), :], STEP * PACK), found).astype(BF16)
        for o in range(STEP):
            gather[pl.ds(boxes + fives, PACK), pl.ds(o * width, width)] = placed[
                o * PACK : (o + 1) * PACK
            ]
        ops = mats[pl.ds(step * STEP, STEP)].reshape(STEP * width, width)
        total[...] += dot(gather[...], ops)

    parts = out_ref.shape[0]
    six, five, four = boxes // parts, fives // parts, fours // parts
    for part in range(parts):
        out_ref[part, pl.ds(0, six), :] = total[pl.ds(part * six, six), :].astype(BF16)
        tail = jnp.concatenate(
            [
                total[pl.ds(boxes + part * five, five), :] * 0.5,
                total[pl.ds(boxes + fives + part * four, four), :] * 0.25,
                jnp.zeros((PACK - five - four, width), F32),
            ],
            axis=0,
        )
        out_ref[part, pl.ds(six, PACK), :] = tail.astype(BF16)


def combine_kernel(sizes, part_ref, down_ref, out_ref, got, wide, send, recv):
    n_m, n_s = sizes
    m, s = lax.axis_index("morton"), lax.axis_index("sub")
    barrier = pltpu.get_barrier_semaphore()
    for k in range(1, n_s):
        pl.semaphore_signal(barrier, inc=1, device_id=(m, (s + k) % n_s), device_id_type=MESH)
    pl.semaphore_wait(barrier, n_s - 1)

    def part_copy(k):
        other = (s + k) % n_s
        return pltpu.make_async_remote_copy(
            src_ref=part_ref.at[other],
            dst_ref=got.at[k],
            send_sem=send.at[k],
            recv_sem=recv.at[k],
            device_id=(m, other),
            device_id_type=MESH,
        )

    for k in range(1, n_s):
        part_copy(k).start()
    total = part_ref[s].astype(F32)
    for k in range(1, n_s):
        part_copy(k).wait_recv()
        total = total + got[k].astype(F32)
    six = out_ref.shape[0]
    four = total[six + 8 : six + 9, :].astype(BF16)
    spread = [dot(four, down_ref[c]) for c in range(8)]
    five = (total[six : six + 8, :] + jnp.concatenate(spread, axis=0)).astype(BF16)
    for c in range(8):
        wide[pl.ds(c, six // 8, stride=8), :] = dot(five, down_ref[c])
    out_ref[...] = (wide[...] + total[:six, :]).astype(BF16)
    for k in range(1, n_s):
        part_copy(k).wait_send()


VMEM = pl.BlockSpec(memory_space=pltpu.VMEM)


def local(sizes, mult, trans, up, down, t6, s6, c6, t5, s5, c5, t4, s4, c4):
    n_m, n_s = sizes
    quarter, width = mult.shape
    boxes = quarter * n_s
    slots = GROUP * n_s
    near, coarse = pl.pallas_call(
        functools.partial(exchange_kernel, sizes),
        out_shape=(
            jax.ShapeDtypeStruct((3 * n_s, quarter, width), BF16),
            jax.ShapeDtypeStruct((slots, PACK, width), BF16),
        ),
        in_specs=[VMEM] * 2,
        out_specs=(VMEM, VMEM),
        scratch_shapes=[
            pltpu.VMEM((quarter, width), F32),
            pltpu.VMEM((PACK, width), BF16),
            pltpu.SemaphoreType.DMA((3 * n_s,)),
            pltpu.SemaphoreType.DMA((3 * n_s,)),
            pltpu.SemaphoreType.DMA((slots,)),
            pltpu.SemaphoreType.DMA((slots,)),
        ],
        compiler_params=pltpu.CompilerParams(collective_id=0, has_side_effects=True),
        name="exchange",
    )(mult, up)

    n_ops = trans.shape[0]
    padded = -(-n_ops // STEP) * STEP
    rows = boxes + boxes // 8 + PACK
    parts = pl.pallas_call(
        functools.partial(translate_kernel, n_m),
        out_shape=jax.ShapeDtypeStruct((n_s, quarter + PACK, width), BF16),
        in_specs=[VMEM, VMEM, pl.BlockSpec(memory_space=pl.ANY)] + [VMEM] * 9,
        out_specs=VMEM,
        scratch_shapes=[
            pltpu.VMEM((padded, width, width), BF16),
            pltpu.VMEM((3 * width, boxes), BF16),
            pltpu.VMEM((width, slots * 8), BF16),
            pltpu.VMEM((width, slots), BF16),
            pltpu.VMEM((padded, t6.shape[2]), F32),
            pltpu.VMEM((padded, t6.shape[2]), F32),
            pltpu.VMEM((padded, t6.shape[2]), F32),
            pltpu.VMEM((padded // 8, 8 * t5.shape[2]), F32),
            pltpu.VMEM((padded // 8, 8 * t5.shape[2]), F32),
            pltpu.VMEM((padded // STEP, STEP * t4.shape[2]), F32),
            pltpu.VMEM((padded // STEP, STEP * t4.shape[2]), F32),
            pltpu.VMEM((rows, STEP * width), BF16),
            pltpu.VMEM((rows, width), F32),
            pltpu.SemaphoreType.DMA,
        ],
        compiler_params=pltpu.CompilerParams(vmem_limit_bytes=32 * 1024 * 1024),
        name="translate",
    )(near, coarse, trans, t6, s6, c6, t5, s5, c5, t4, s4, c4)

    return pl.pallas_call(
        functools.partial(combine_kernel, sizes),
        out_shape=jax.ShapeDtypeStruct((quarter, width), BF16),
        in_specs=[VMEM] * 2,
        out_specs=VMEM,
        scratch_shapes=[
            pltpu.VMEM((n_s, quarter + PACK, width), BF16),
            pltpu.VMEM((quarter, width), F32),
            pltpu.SemaphoreType.DMA((n_s,)),
            pltpu.SemaphoreType.DMA((n_s,)),
        ],
        compiler_params=pltpu.CompilerParams(collective_id=1, has_side_effects=True),
        name="combine",
    )(parts, down)


def solution(mesh):
    sizes = (mesh.shape["morton"], mesh.shape["sub"])
    placed = (
        P(("morton", "sub"), None),
        P("sub", None, None),
        P(),
        P(),
        P("morton", "sub", None),
        P("morton", "sub", None),
        P("morton", "sub"),
        P("morton", "sub", None),
        P("morton", "sub", None),
        P("morton", "sub"),
        P("morton", "sub", None),
        P("morton", "sub", None),
        P("morton", "sub"),
    )
    return jax.shard_map(
        functools.partial(local, sizes),
        mesh=mesh,
        in_specs=placed,
        out_specs=P(("morton", "sub"), None),
        check_vma=False,
    )
```

```python
import functools

import jax
import jax.numpy as jnp
from jax import lax
from jax.experimental import pallas as pl
from jax.experimental.pallas import tpu as pltpu
from jax.sharding import PartitionSpec as P

BF16 = jnp.bfloat16
F32 = jnp.float32
MESH = pl.DeviceIdType.MESH
GROUP = 8
PACK = 16
STEP = 16


def dot(a, b):
    return jnp.dot(a, b, preferred_element_type=F32)


def dot_nt(a, b):
    return lax.dot_general(a, b, (((1,), (1,)), ((), ())), preferred_element_type=F32)


def column_of(row, height):
    width = row.shape[1]
    at = lax.broadcasted_iota(jnp.int32, (height, width), 0)
    on = lax.broadcasted_iota(jnp.int32, (height, width), 1)
    return jnp.sum(jnp.where(at == on, row, 0.0), axis=1, keepdims=True)


def folded(values, per_row):
    n, cap = values.shape
    lanes = per_row * cap
    j = lax.broadcasted_iota(jnp.int32, (cap, lanes), 0)
    lane = lax.broadcasted_iota(jnp.int32, (cap, lanes), 1)
    spread = jnp.where(lane % cap == j, 1.0, 0.0).astype(BF16)
    wide = dot(values.astype(BF16), spread)
    at = lax.broadcasted_iota(jnp.int32, (n, lanes), 0)
    on = lax.broadcasted_iota(jnp.int32, (n, lanes), 1)
    wide = jnp.where(at % per_row == on // cap, wide, 0.0).astype(BF16)
    out = lax.broadcasted_iota(jnp.int32, (n // per_row, n), 0)
    src = lax.broadcasted_iota(jnp.int32, (n // per_row, n), 1)
    return dot(jnp.where(src // per_row == out, 1.0, 0.0).astype(BF16), wide)


def one_hot(ids, row):
    height, lanes = ids.shape
    rows = jnp.broadcast_to(row, (16, lanes)).astype(BF16)
    same = ids.reshape(height // 16, 16, lanes) == rows[None]
    one, none = jnp.ones((), BF16), jnp.zeros((), BF16)
    return jnp.where(same, one, none).reshape(height, lanes)


def wrapped(value, size):
    return jnp.where(value >= size, value - size, value)


def upward_rows(children, up, wide):
    parents = children.shape[0] // 8
    wide[...] = children.astype(F32)
    rows = [wide[pl.ds(c, parents, stride=8), :] for c in range(8)]
    ops = up.reshape(-1, up.shape[2])
    five = dot(jnp.concatenate(rows, axis=1).astype(BF16), ops).astype(BF16).astype(F32)
    row = jnp.concatenate([five[c : c + 1, :] for c in range(8)], axis=1).astype(BF16)
    pad = jnp.zeros((PACK - parents - 1, five.shape[1]), F32)
    return jnp.concatenate([five, dot(row, ops), pad], axis=0).astype(BF16)


def kernel(
    sizes, mult_hbm, tr_hbm, up_hbm, down_hbm, t6_hbm, s6_hbm, c6_hbm, t5_hbm, s5_hbm, c5_hbm,
    t4_hbm, s4_hbm, c4_hbm, out_ref,
    near, coarse, mats, up, down, t6, s6, c6, t5, s5, c5, t4, s4, c4,
    wide, mt, c5t, c4t, tg6, sr6, bl6, tg5, sr5, tg4, sr4,
    picks, places, apart, gather, parts, got,
    load, near_send, near_recv, pass_send, pack_send, pack_recv, join_send, join_recv,
    part_send, part_recv,
):
    n_m, n_s = sizes
    n_ops, width = tr_hbm.shape[0], tr_hbm.shape[2]
    padded = mats.shape[0]
    quarter = near.shape[1]
    boxes = quarter * n_s
    fives, fours = boxes // 8, boxes // 64
    cap6, cap5, cap4 = t6.shape[2], t5.shape[1], t4.shape[1]
    m, s = lax.axis_index("morton"), lax.axis_index("sub")
    base = m * 0 if n_m == GROUP else m // GROUP * GROUP
    here = m - base
    following = wrapped(m + 1, n_m)
    previous = jnp.where(m == 0, n_m - 1, m - 1)

    barrier = pltpu.get_barrier_semaphore()

    def greet(peer):
        pl.semaphore_signal(barrier, inc=1, device_id=peer, device_id_type=MESH)

    for k in range(1, n_s):
        greet((m, wrapped(s + k, n_s)))
    for k in range(1, GROUP):
        greet((base + wrapped(here + k, GROUP), s))
    expected = n_s - 1 + GROUP - 1
    if n_m > GROUP:
        greet((following, s))
        greet((previous, s))
        expected = expected + 2

    own = near.at[n_s + s]
    pairs = [
        (mult_hbm, own), (up_hbm, up), (c6_hbm, c6), (t6_hbm, t6), (s6_hbm, s6),
        (c5_hbm, c5), (t5_hbm, t5), (s5_hbm, s5), (c4_hbm, c4), (t4_hbm, t4), (s4_hbm, s4),
        (tr_hbm, mats.at[pl.ds(0, n_ops)]), (down_hbm, down),
    ]
    loads = [pltpu.make_async_copy(a, b, load.at[i]) for i, (a, b) in enumerate(pairs)]
    for copy in loads:
        copy.start()

    def remote(src, dst, send, recv, peer):
        return pltpu.make_async_remote_copy(
            src_ref=src, dst_ref=dst, send_sem=send, recv_sem=recv,
            device_id=peer, device_id_type=MESH,
        )

    def halo_copy(side):
        slot = side * 2 * n_s + s
        return remote(
            own, near.at[slot], near_send.at[side], near_recv.at[slot],
            (previous if side else following, s),
        )

    def sub_copy(k, there):
        other = wrapped(s + k, n_s)
        slot = n_s + (other if there else s)
        return remote(
            own, near.at[slot], near_send.at[2 + k], near_recv.at[slot], (m, other)
        )

    def pass_copy(side, k, there):
        other = wrapped(s + k, n_s)
        slot = side * 2 * n_s + (other if there else s)
        return remote(
            near.at[slot], near.at[slot], pass_send.at[side * n_s + k], near_recv.at[slot],
            (m, other),
        )

    def pack_copy(k, there):
        other = wrapped(s + k, n_s)
        slot = coarse.at[here, other if there else s]
        return remote(
            slot, slot, pack_send.at[k], pack_recv.at[other if there else s], (m, other)
        )

    def join_copy(k, there):
        other = wrapped(here + k, GROUP)
        slot = other if there else here
        return remote(
            coarse.at[slot], coarse.at[slot], join_send.at[k], join_recv.at[slot],
            (base + other, s),
        )

    def part_copy(k):
        other = wrapped(s + k, n_s)
        return remote(
            parts.at[other], got.at[k], part_send.at[k], part_recv.at[k], (m, other)
        )

    loads[0].wait()
    pl.semaphore_wait(barrier, expected)
    for side in range(2):
        halo_copy(side).start()
    for k in range(1, n_s):
        sub_copy(k, False).start()
    loads[1].wait()
    coarse[here, s] = upward_rows(near[n_s + s], up[...], wide)
    for k in range(1, n_s):
        pack_copy(k, False).start()

    for copy in loads[2:11]:
        copy.wait()

    def filled(values, fill):
        if padded == n_ops:
            return values
        more = jnp.full((padded - n_ops, values.shape[1]), fill, F32)
        return jnp.concatenate([values, more], axis=0)

    lane = lax.broadcasted_iota(jnp.int32, (n_ops, cap6), 1).astype(F32)
    live = lane < column_of(c6[...].astype(F32), n_ops)
    tg6[...] = filled(jnp.where(live, t6[:, 0, :].astype(F32), -1.0), -1.0)
    source = s6[:, 0, :]
    block = jnp.where(source >= boxes, 1, 0) + jnp.where(source >= 2 * boxes, 1, 0)
    sr6[...] = filled((source - block * boxes).astype(F32), 0.0)
    bl6[...] = filled(block.astype(F32), 0.0)

    at = lax.broadcasted_iota(jnp.int32, (padded, n_ops), 0)
    on = lax.broadcasted_iota(jnp.int32, (padded, n_ops), 1)
    turn = jnp.where(at == on, 1.0, 0.0).astype(BF16)

    def keys(t_ref, c_ref, per_row, height):
        cap = t_ref.shape[1]
        slot = lax.broadcasted_iota(jnp.int32, (cap, n_ops), 0)
        alive = jnp.where(slot < c_ref[...], t_ref[0] + 1, 0).astype(F32).astype(BF16)
        raw = folded(dot_nt(turn, alive), per_row)
        lane = lax.broadcasted_iota(jnp.int32, raw.shape, 1) // cap
        return jnp.where(raw > 0.0, raw - 1.0 + (lane * height).astype(F32), -1.0)

    def sources(s_ref, per_row):
        return folded(dot_nt(turn, s_ref[0].astype(F32).astype(BF16)), per_row)

    tg5[...] = keys(t5, c5, 8, fives)
    sr5[...] = sources(s5, 8)
    tg4[...] = keys(t4, c4, STEP, PACK)
    sr4[...] = sources(s4, STEP)
    for o in range(n_ops, padded):
        mats[o] = jnp.zeros(mats.shape[1:], BF16)
    apart[...] = jnp.zeros(apart.shape, BF16)

    for side in range(2):
        halo_copy(side).wait_recv()
        for k in range(1, n_s):
            pass_copy(side, k, False).start()
    for k in range(1, n_s):
        pack_copy(k, True).wait_recv()
    for k in range(1, GROUP):
        join_copy(k, False).start()
    for k in range(1, n_s):
        sub_copy(k, True).wait_recv()
    for side in range(2):
        for k in range(1, n_s):
            pass_copy(side, k, True).wait_recv()

    r = lax.broadcasted_iota(jnp.int32, (width, width), 0)
    c = lax.broadcasted_iota(jnp.int32, (width, width), 1)
    eye = jnp.where(r == c, 1.0, 0.0).astype(BF16)
    nearby = near[...].reshape(3, boxes, width)
    for block in range(3):
        rows = dot_nt(eye, nearby[block])
        if block == 0:
            rows = jnp.where(m == 0, 0.0, rows)
        if block == 2:
            rows = jnp.where(m == n_m - 1, 0.0, rows)
        mt[pl.ds(block * width, width), :] = rows.astype(BF16)

    ids = lax.broadcasted_iota(jnp.int32, (boxes, cap6), 0).astype(F32).astype(BF16)

    @pl.loop(0, padded // STEP)
    def _(step):
        def mark(pair):
            for half in range(2):
                o = step * STEP + 2 * pair + half
                lanes = pl.ds((2 * pair + half) * cap6, cap6)
                picks[:, lanes] = one_hot(ids, sr6[pl.ds(o, 1), :])
                places[:, lanes] = one_hot(ids, tg6[pl.ds(o, 1), :])

        def pick(pair):
            found = dot(mt[...], picks[:, pl.ds(2 * pair * cap6, 2 * cap6)])
            for half in range(2):
                head = bl6[pl.ds(step * STEP + 2 * pair + half, 1), :]
                piece = found[:, half * cap6 : (half + 1) * cap6]
                apart[pair, pl.ds(half * width, width), pl.ds(half * cap6, cap6)] = jnp.where(
                    head == 0.0,
                    piece[:width],
                    jnp.where(head == 1.0, piece[width : 2 * width], piece[2 * width :]),
                ).astype(BF16)

        def place(pair):
            placed = dot_nt(places[:, pl.ds(2 * pair * cap6, 2 * cap6)], apart[pair])
            lanes = pl.ds(
                pl.multiple_of(step * STEP * width + 2 * pair * width, 2 * width), 2 * width
            )
            gather[pl.ds(0, boxes), lanes] = placed.astype(BF16)

        for turn in range(STEP // 2 + 2):
            if turn >= 2:
                place(turn - 2)
            if 1 <= turn <= STEP // 2:
                pick(turn - 1)
            if turn < STEP // 2:
                mark(turn)

    for k in range(1, GROUP):
        join_copy(k, True).wait_recv()
    slots = GROUP * n_s
    packed = dot_nt(eye, coarse[...].reshape(slots * PACK, width)).astype(BF16)
    q = lax.broadcasted_iota(jnp.int32, (slots * PACK, slots * 8), 0)
    p = lax.broadcasted_iota(jnp.int32, (slots * PACK, slots * 8), 1)
    c5t[...] = dot(packed, jnp.where(q == p // 8 * PACK + p % 8, 1.0, 0.0).astype(BF16)).astype(BF16)
    q = lax.broadcasted_iota(jnp.int32, (slots * PACK, slots), 0)
    p = lax.broadcasted_iota(jnp.int32, (slots * PACK, slots), 1)
    c4t[...] = dot(packed, jnp.where(q == p * PACK + 8, 1.0, 0.0).astype(BF16)).astype(BF16)

    def numbers(height, lanes):
        return lax.broadcasted_iota(jnp.int32, (height, lanes), 0).astype(F32).astype(BF16)

    source5, target5 = numbers(slots * 8, 8 * cap5), numbers(8 * fives, 8 * cap5)
    source4, target4 = numbers(slots, STEP * cap4), numbers(STEP * PACK, STEP * cap4)

    @pl.loop(0, padded // STEP)
    def _(step):
        def at(o):
            return pl.ds(pl.multiple_of(step * STEP * width + o * width, width), width)

        for half in range(STEP // 8):
            row = step * (STEP // 8) + half
            found = dot(c5t[...], one_hot(source5, sr5[pl.ds(row, 1), :])).astype(BF16)
            placed = dot_nt(one_hot(target5, tg5[pl.ds(row, 1), :]), found).astype(BF16)
            for o in range(8):
                gather[pl.ds(boxes, fives), at(half * 8 + o)] = placed[o * fives : (o + 1) * fives]
        found = dot(c4t[...], one_hot(source4, sr4[pl.ds(step, 1), :])).astype(BF16)
        placed = dot_nt(one_hot(target4, tg4[pl.ds(step, 1), :]), found).astype(BF16)
        for o in range(STEP):
            gather[pl.ds(boxes + fives, PACK), at(o)] = placed[o * PACK : (o + 1) * PACK]

    loads[11].wait()
    total = dot(gather[...], mats[...].reshape(padded * width, width))

    six, five, four = boxes // n_s, fives // n_s, fours // n_s
    for part in range(n_s):
        parts[part, pl.ds(0, six), :] = total[part * six : (part + 1) * six].astype(BF16)
        low = boxes + fives + part * four
        tail = jnp.concatenate(
            [
                total[boxes + part * five : boxes + (part + 1) * five] * 0.5,
                total[low : low + four] * 0.25,
                jnp.zeros((PACK - five - four, width), F32),
            ],
            axis=0,
        )
        parts[part, pl.ds(six, PACK), :] = tail.astype(BF16)
    for k in range(1, n_s):
        part_copy(k).start()
    loads[12].wait()
    whole = parts[s].astype(F32)
    for k in range(1, n_s):
        part_copy(k).wait_recv()
        whole = whole + got[k].astype(F32)
    row = whole[six + five : six + five + 1, :].astype(BF16)
    spread = [dot(row, down[c]) for c in range(8)]
    mid = (whole[six : six + five, :] + jnp.concatenate(spread, axis=0)).astype(BF16)
    for c in range(8):
        wide[pl.ds(c, six // 8, stride=8), :] = dot(mid, down[c])
    out_ref[...] = (wide[...] + whole[:six, :]).astype(BF16)

    for side in range(2):
        halo_copy(side).wait_send()
        for k in range(1, n_s):
            pass_copy(side, k, False).wait_send()
    for k in range(1, n_s):
        sub_copy(k, False).wait_send()
        pack_copy(k, False).wait_send()
        part_copy(k).wait_send()
    for k in range(1, GROUP):
        join_copy(k, False).wait_send()


def local(sizes, mult, trans, up, down, t6, s6, c6, t5, s5, c5, t4, s4, c4):
    n_m, n_s = sizes
    quarter, width = mult.shape
    boxes = quarter * n_s
    slots = GROUP * n_s
    n_ops = trans.shape[0]
    padded = -(-n_ops // STEP) * STEP
    rows = boxes + boxes // 8 + PACK
    cap6, cap5, cap4 = t6.shape[2], t5.shape[2], t4.shape[2]
    t6, s6 = jnp.swapaxes(t6, 0, 1), jnp.swapaxes(s6, 0, 1)
    t5, s5, t4, s4 = (jnp.swapaxes(x, 1, 2) for x in (t5, s5, t4, s4))
    index = [pltpu.VMEM(x.shape, x.dtype) for x in (t6, s6, c6, t5, s5, c5, t4, s4, c4)]
    sems = pltpu.SemaphoreType.DMA
    return pl.pallas_call(
        functools.partial(kernel, sizes),
        out_shape=jax.ShapeDtypeStruct((quarter, width), BF16),
        in_specs=[pl.BlockSpec(memory_space=pl.ANY)] * 13,
        out_specs=pl.BlockSpec(memory_space=pltpu.VMEM),
        scratch_shapes=[
            pltpu.VMEM((3 * n_s, quarter, width), BF16),
            pltpu.VMEM((GROUP, n_s, PACK, width), BF16),
            pltpu.VMEM((padded, width, width), BF16),
            pltpu.VMEM(up.shape, BF16),
            pltpu.VMEM(down.shape, BF16),
            *index,
            pltpu.VMEM((quarter, width), F32),
            pltpu.VMEM((3 * width, boxes), BF16),
            pltpu.VMEM((width, slots * 8), BF16),
            pltpu.VMEM((width, slots), BF16),
            pltpu.VMEM((padded, cap6), F32),
            pltpu.VMEM((padded, cap6), F32),
            pltpu.VMEM((padded, cap6), F32),
            pltpu.VMEM((padded // 8, 8 * cap5), F32),
            pltpu.VMEM((padded // 8, 8 * cap5), F32),
            pltpu.VMEM((padded // STEP, STEP * cap4), F32),
            pltpu.VMEM((padded // STEP, STEP * cap4), F32),
            pltpu.VMEM((boxes, STEP * cap6), BF16),
            pltpu.VMEM((boxes, STEP * cap6), BF16),
            pltpu.VMEM((STEP // 2, 2 * width, 2 * cap6), BF16),
            pltpu.VMEM((rows, padded * width), BF16),
            pltpu.VMEM((n_s, quarter + PACK, width), BF16),
            pltpu.VMEM((n_s, quarter + PACK, width), BF16),
            sems((13,)),
            sems((2 + n_s,)),
            sems((3 * n_s,)),
            sems((2 * n_s,)),
            sems((n_s,)),
            sems((n_s,)),
            sems((GROUP,)),
            sems((GROUP,)),
            sems((n_s,)),
            sems((n_s,)),
        ],
        compiler_params=pltpu.CompilerParams(
            collective_id=0, has_side_effects=True, vmem_limit_bytes=48 * 1024 * 1024
        ),
        name="far_field",
    )(mult, trans, up, down, t6, s6, c6, t5, s5, c5, t4, s4, c4)


def solution(mesh):
    sizes = (mesh.shape["morton"], mesh.shape["sub"])
    placed = (
        P(("morton", "sub"), None),
        P("sub", None, None),
        P(),
        P(),
        P("morton", "sub", None),
        P("morton", "sub", None),
        P("morton", "sub"),
        P("morton", "sub", None),
        P("morton", "sub", None),
        P("morton", "sub"),
        P("morton", "sub", None),
        P("morton", "sub", None),
        P("morton", "sub"),
    )
    return jax.shard_map(
        functools.partial(local, sizes),
        mesh=mesh,
        in_specs=placed,
        out_specs=P(("morton", "sub"), None),
        check_vma=False,
    )
```

```python
import functools

import jax
import jax.numpy as jnp
from jax import lax
from jax.experimental import pallas as pl
from jax.experimental.pallas import tpu as pltpu
from jax.sharding import PartitionSpec as P

BF16 = jnp.bfloat16
F32 = jnp.float32
MESH = pl.DeviceIdType.MESH
GROUP = 8
PACK = 16
STEP = 16


def dot(a, b):
    return jnp.dot(a, b, preferred_element_type=F32)


def dot_nt(a, b):
    return lax.dot_general(a, b, (((1,), (1,)), ((), ())), preferred_element_type=F32)


def column_of(row, height):
    width = row.shape[1]
    at = lax.broadcasted_iota(jnp.int32, (height, width), 0)
    on = lax.broadcasted_iota(jnp.int32, (height, width), 1)
    return jnp.sum(jnp.where(at == on, row, 0.0), axis=1, keepdims=True)


def folded(values, per_row):
    n, cap = values.shape
    lanes = per_row * cap
    j = lax.broadcasted_iota(jnp.int32, (cap, lanes), 0)
    lane = lax.broadcasted_iota(jnp.int32, (cap, lanes), 1)
    spread = jnp.where(lane % cap == j, 1.0, 0.0).astype(BF16)
    wide = dot(values.astype(BF16), spread)
    at = lax.broadcasted_iota(jnp.int32, (n, lanes), 0)
    on = lax.broadcasted_iota(jnp.int32, (n, lanes), 1)
    wide = jnp.where(at % per_row == on // cap, wide, 0.0).astype(BF16)
    out = lax.broadcasted_iota(jnp.int32, (n // per_row, n), 0)
    src = lax.broadcasted_iota(jnp.int32, (n // per_row, n), 1)
    return dot(jnp.where(src // per_row == out, 1.0, 0.0).astype(BF16), wide)


def one_hot(ids, row):
    height, lanes = ids.shape
    rows = jnp.broadcast_to(row, (16, lanes)).astype(BF16)
    same = ids.reshape(height // 16, 16, lanes) == rows[None]
    one, none = jnp.ones((), BF16), jnp.zeros((), BF16)
    return jnp.where(same, one, none).reshape(height, lanes)


def wrapped(value, size):
    return jnp.where(value >= size, value - size, value)


def upward_rows(children, up, wide):
    parents = children.shape[0] // 8
    wide[...] = children.astype(F32)
    rows = [wide[pl.ds(c, parents, stride=8), :] for c in range(8)]
    ops = up.reshape(-1, up.shape[2])
    five = dot(jnp.concatenate(rows, axis=1).astype(BF16), ops).astype(BF16).astype(F32)
    row = jnp.concatenate([five[c : c + 1, :] for c in range(8)], axis=1).astype(BF16)
    pad = jnp.zeros((PACK - parents - 1, five.shape[1]), F32)
    return jnp.concatenate([five, dot(row, ops), pad], axis=0).astype(BF16)


def kernel(
    sizes, mult_hbm, tr_hbm, up_hbm, down_hbm, t6_hbm, s6_hbm, c6_hbm, t5_hbm, s5_hbm, c5_hbm,
    t4_hbm, s4_hbm, c4_hbm, out_ref,
    near, coarse, mats, up, down, t6, s6, c6, t5, s5, c5, t4, s4, c4,
    wide, mt, c5t, c4t, tg6, sr6, bl6, tg5, sr5, tg4, sr4,
    picks, places, apart, gather, parts, got, choose5, choose4,
    load, near_send, near_recv, pass_send, pack_send, pack_recv, join_send, join_recv,
    part_send, part_recv,
):
    n_m, n_s = sizes
    n_ops, width = tr_hbm.shape[0], tr_hbm.shape[2]
    padded = mats.shape[0]
    quarter = near.shape[1]
    boxes = quarter * n_s
    fives, fours = boxes // 8, boxes // 64
    cap6, cap5, cap4 = t6.shape[2], t5.shape[1], t4.shape[1]
    m, s = lax.axis_index("morton"), lax.axis_index("sub")
    base = m * 0 if n_m == GROUP else m // GROUP * GROUP
    here = m - base
    following = wrapped(m + 1, n_m)
    previous = jnp.where(m == 0, n_m - 1, m - 1)

    barrier = pltpu.get_barrier_semaphore()

    def greet(peer):
        pl.semaphore_signal(barrier, inc=1, device_id=peer, device_id_type=MESH)

    for k in range(1, n_s):
        greet((m, wrapped(s + k, n_s)))
    for k in range(1, GROUP):
        greet((base + wrapped(here + k, GROUP), s))
    expected = n_s - 1 + GROUP - 1
    if n_m > GROUP:
        greet((following, s))
        greet((previous, s))
        expected = expected + 2

    own = near.at[n_s + s]
    pairs = [
        (mult_hbm, own), (up_hbm, up), (c6_hbm, c6), (t6_hbm, t6), (s6_hbm, s6),
        (c5_hbm, c5), (t5_hbm, t5), (s5_hbm, s5), (c4_hbm, c4), (t4_hbm, t4), (s4_hbm, s4),
        (tr_hbm, mats.at[pl.ds(0, n_ops)]), (down_hbm, down),
    ]
    loads = [pltpu.make_async_copy(a, b, load.at[i]) for i, (a, b) in enumerate(pairs)]
    for copy in loads:
        copy.start()

    def remote(src, dst, send, recv, peer):
        return pltpu.make_async_remote_copy(
            src_ref=src, dst_ref=dst, send_sem=send, recv_sem=recv,
            device_id=peer, device_id_type=MESH,
        )

    def halo_copy(side):
        slot = side * 2 * n_s + s
        return remote(
            own, near.at[slot], near_send.at[side], near_recv.at[slot],
            (previous if side else following, s),
        )

    def sub_copy(k, there):
        other = wrapped(s + k, n_s)
        slot = n_s + (other if there else s)
        return remote(
            own, near.at[slot], near_send.at[2 + k], near_recv.at[slot], (m, other)
        )

    def pass_copy(side, k, there):
        other = wrapped(s + k, n_s)
        slot = side * 2 * n_s + (other if there else s)
        return remote(
            near.at[slot], near.at[slot], pass_send.at[side * n_s + k], near_recv.at[slot],
            (m, other),
        )

    def pack_copy(k, there):
        other = wrapped(s + k, n_s)
        slot = coarse.at[here, other if there else s]
        return remote(
            slot, slot, pack_send.at[k], pack_recv.at[other if there else s], (m, other)
        )

    def join_copy(k, there):
        other = wrapped(here + k, GROUP)
        slot = other if there else here
        return remote(
            coarse.at[slot], coarse.at[slot], join_send.at[k], join_recv.at[slot],
            (base + other, s),
        )

    def part_copy(k):
        other = wrapped(s + k, n_s)
        return remote(
            parts.at[other], got.at[k], part_send.at[k], part_recv.at[k], (m, other)
        )

    loads[0].wait()
    pl.semaphore_wait(barrier, expected)
    for side in range(2):
        halo_copy(side).start()
    for k in range(1, n_s):
        sub_copy(k, False).start()
    loads[1].wait()
    coarse[here, s] = upward_rows(near[n_s + s], up[...], wide)
    for k in range(1, n_s):
        pack_copy(k, False).start()

    for copy in loads[2:11]:
        copy.wait()

    def filled(values, fill):
        if padded == n_ops:
            return values
        more = jnp.full((padded - n_ops, values.shape[1]), fill, F32)
        return jnp.concatenate([values, more], axis=0)

    lane = lax.broadcasted_iota(jnp.int32, (n_ops, cap6), 1).astype(F32)
    live = lane < column_of(c6[...].astype(F32), n_ops)
    tg6[...] = filled(jnp.where(live, t6[:, 0, :].astype(F32), -1.0), -1.0)
    source = s6[:, 0, :]
    block = jnp.where(source >= boxes, 1, 0) + jnp.where(source >= 2 * boxes, 1, 0)
    sr6[...] = filled((source - block * boxes).astype(F32), 0.0)
    bl6[...] = filled(block.astype(F32), 0.0)

    at = lax.broadcasted_iota(jnp.int32, (padded, n_ops), 0)
    on = lax.broadcasted_iota(jnp.int32, (padded, n_ops), 1)
    turn = jnp.where(at == on, 1.0, 0.0).astype(BF16)

    def keys(t_ref, c_ref, per_row, height):
        cap = t_ref.shape[1]
        slot = lax.broadcasted_iota(jnp.int32, (cap, n_ops), 0)
        alive = jnp.where(slot < c_ref[...], t_ref[0] + 1, 0).astype(F32).astype(BF16)
        raw = folded(dot_nt(turn, alive), per_row)
        lane = lax.broadcasted_iota(jnp.int32, raw.shape, 1) // cap
        return jnp.where(raw > 0.0, raw - 1.0 + (lane * height).astype(F32), -1.0)

    def sources(s_ref, per_row):
        return folded(dot_nt(turn, s_ref[0].astype(F32).astype(BF16)), per_row)

    tg5[...] = keys(t5, c5, 8, fives)
    sr5[...] = sources(s5, 8)
    tg4[...] = keys(t4, c4, STEP, PACK)
    sr4[...] = sources(s4, STEP)

    for side in range(2):
        halo_copy(side).wait_recv()
        for k in range(1, n_s):
            pass_copy(side, k, False).start()
    for k in range(1, n_s):
        pack_copy(k, True).wait_recv()
    for k in range(1, GROUP):
        join_copy(k, False).start()
    slots = GROUP * n_s
    q = lax.broadcasted_iota(jnp.int32, (slots * PACK, slots * 8), 0)
    p = lax.broadcasted_iota(jnp.int32, (slots * PACK, slots * 8), 1)
    choose5[...] = jnp.where(q == p // 8 * PACK + p % 8, 1.0, 0.0).astype(BF16)
    q = lax.broadcasted_iota(jnp.int32, (slots * PACK, slots), 0)
    p = lax.broadcasted_iota(jnp.int32, (slots * PACK, slots), 1)
    choose4[...] = jnp.where(q == p * PACK + 8, 1.0, 0.0).astype(BF16)

    apart[...] = jnp.zeros(apart.shape, BF16)
    for o in range(n_ops, padded):
        mats[o] = jnp.zeros(mats.shape[1:], BF16)
    ids = lax.broadcasted_iota(jnp.int32, (boxes, cap6), 0).astype(F32).astype(BF16)

    @pl.loop(0, padded // STEP)
    def _(step):
        for j in range(STEP):
            lanes = pl.ds(pl.multiple_of(step * STEP * cap6 + j * cap6, cap6), cap6)
            picks[:, lanes] = one_hot(ids, sr6[pl.ds(step * STEP + j, 1), :])
            places[:, lanes] = one_hot(ids, tg6[pl.ds(step * STEP + j, 1), :])

    r = lax.broadcasted_iota(jnp.int32, (width, width), 0)
    c = lax.broadcasted_iota(jnp.int32, (width, width), 1)
    eye = jnp.where(r == c, 1.0, 0.0).astype(BF16)

    for k in range(1, n_s):
        sub_copy(k, True).wait_recv()
    for side in range(2):
        for k in range(1, n_s):
            pass_copy(side, k, True).wait_recv()

    nearby = near[...].reshape(3, boxes, width)
    for block in range(3):
        rows = dot_nt(eye, nearby[block])
        if block == 0:
            rows = jnp.where(m == 0, 0.0, rows)
        if block == 2:
            rows = jnp.where(m == n_m - 1, 0.0, rows)
        mt[pl.ds(block * width, width), :] = rows.astype(BF16)

    @pl.loop(0, padded // STEP)
    def _(step):
        def both(pair):
            start = step * STEP * cap6 + 2 * pair * cap6
            return pl.ds(pl.multiple_of(start, 2 * cap6), 2 * cap6)

        def pick(pair):
            found = dot(mt[...], picks[:, both(pair)]).astype(BF16)
            for half in range(2):
                head = bl6[pl.ds(step * STEP + 2 * pair + half, 1), :]
                head = jnp.broadcast_to(head, (16, cap6)).astype(BF16)[None]
                piece = found[:, half * cap6 : (half + 1) * cap6].reshape(3, width // 16, 16, cap6)
                chosen = jnp.where(head == 1.0, piece[1], piece[2])
                chosen = jnp.where(head == 0.0, piece[0], chosen)
                apart[pair, pl.ds(half * width, width), pl.ds(half * cap6, cap6)] = (
                    chosen.reshape(width, cap6)
                )

        def place(pair):
            placed = dot_nt(places[:, both(pair)], apart[pair])
            start = step * STEP * width + 2 * pair * width
            lanes = pl.ds(pl.multiple_of(start, 2 * width), 2 * width)
            gather[pl.ds(0, boxes), lanes] = placed.astype(BF16)

        for turn in range(STEP // 2 + 1):
            if turn >= 1:
                place(turn - 1)
            if turn < STEP // 2:
                pick(turn)

    for k in range(1, GROUP):
        join_copy(k, True).wait_recv()
    packed = dot_nt(eye, coarse[...].reshape(slots * PACK, width)).astype(BF16)
    c5t[...] = dot(packed, choose5[...]).astype(BF16)
    c4t[...] = dot(packed, choose4[...]).astype(BF16)

    def numbers(height, lanes):
        return lax.broadcasted_iota(jnp.int32, (height, lanes), 0).astype(F32).astype(BF16)

    source5, target5 = numbers(slots * 8, 8 * cap5), numbers(8 * fives, 8 * cap5)
    source4, target4 = numbers(slots, STEP * cap4), numbers(STEP * PACK, STEP * cap4)

    @pl.loop(0, padded // STEP)
    def _(step):
        def at(o):
            return pl.ds(pl.multiple_of(step * STEP * width + o * width, width), width)

        for half in range(STEP // 8):
            row = step * (STEP // 8) + half
            found = dot(c5t[...], one_hot(source5, sr5[pl.ds(row, 1), :])).astype(BF16)
            placed = dot_nt(one_hot(target5, tg5[pl.ds(row, 1), :]), found).astype(BF16)
            for o in range(8):
                gather[pl.ds(boxes, fives), at(half * 8 + o)] = placed[o * fives : (o + 1) * fives]
        found = dot(c4t[...], one_hot(source4, sr4[pl.ds(step, 1), :])).astype(BF16)
        placed = dot_nt(one_hot(target4, tg4[pl.ds(step, 1), :]), found).astype(BF16)
        for o in range(STEP):
            gather[pl.ds(boxes + fives, PACK), at(o)] = placed[o * PACK : (o + 1) * PACK]

    loads[11].wait()
    total = dot(gather[...], mats[...].reshape(padded * width, width))

    six, five, four = boxes // n_s, fives // n_s, fours // n_s
    for part in range(n_s):
        parts[part, pl.ds(0, six), :] = total[part * six : (part + 1) * six].astype(BF16)
        low = boxes + fives + part * four
        tail = jnp.concatenate(
            [
                total[boxes + part * five : boxes + (part + 1) * five] * 0.5,
                total[low : low + four] * 0.25,
                jnp.zeros((PACK - five - four, width), F32),
            ],
            axis=0,
        )
        parts[part, pl.ds(six, PACK), :] = tail.astype(BF16)
    for k in range(1, n_s):
        part_copy(k).start()
    loads[12].wait()
    whole = parts[s].astype(F32)
    for k in range(1, n_s):
        part_copy(k).wait_recv()
        whole = whole + got[k].astype(F32)
    row = whole[six + five : six + five + 1, :].astype(BF16)
    spread = [dot(row, down[c]) for c in range(8)]
    mid = (whole[six : six + five, :] + jnp.concatenate(spread, axis=0)).astype(BF16)
    for c in range(8):
        wide[pl.ds(c, six // 8, stride=8), :] = dot(mid, down[c])
    out_ref[...] = (wide[...] + whole[:six, :]).astype(BF16)

    for side in range(2):
        halo_copy(side).wait_send()
        for k in range(1, n_s):
            pass_copy(side, k, False).wait_send()
    for k in range(1, n_s):
        sub_copy(k, False).wait_send()
        pack_copy(k, False).wait_send()
        part_copy(k).wait_send()
    for k in range(1, GROUP):
        join_copy(k, False).wait_send()


def local(sizes, mult, trans, up, down, t6, s6, c6, t5, s5, c5, t4, s4, c4):
    n_m, n_s = sizes
    quarter, width = mult.shape
    boxes = quarter * n_s
    slots = GROUP * n_s
    n_ops = trans.shape[0]
    padded = -(-n_ops // STEP) * STEP
    rows = boxes + boxes // 8 + PACK
    cap6, cap5, cap4 = t6.shape[2], t5.shape[2], t4.shape[2]
    t6, s6 = jnp.swapaxes(t6, 0, 1), jnp.swapaxes(s6, 0, 1)
    t5, s5, t4, s4 = (jnp.swapaxes(x, 1, 2) for x in (t5, s5, t4, s4))
    index = [pltpu.VMEM(x.shape, x.dtype) for x in (t6, s6, c6, t5, s5, c5, t4, s4, c4)]
    sems = pltpu.SemaphoreType.DMA
    return pl.pallas_call(
        functools.partial(kernel, sizes),
        out_shape=jax.ShapeDtypeStruct((quarter, width), BF16),
        in_specs=[pl.BlockSpec(memory_space=pltpu.HBM)] * 13,
        out_specs=pl.BlockSpec(memory_space=pltpu.VMEM),
        scratch_shapes=[
            pltpu.VMEM((3 * n_s, quarter, width), BF16),
            pltpu.VMEM((GROUP, n_s, PACK, width), BF16),
            pltpu.VMEM((padded, width, width), BF16),
            pltpu.VMEM(up.shape, BF16),
            pltpu.VMEM(down.shape, BF16),
            *index,
            pltpu.VMEM((quarter, width), F32),
            pltpu.VMEM((3 * width, boxes), BF16),
            pltpu.VMEM((width, slots * 8), BF16),
            pltpu.VMEM((width, slots), BF16),
            pltpu.VMEM((padded, cap6), F32),
            pltpu.VMEM((padded, cap6), F32),
            pltpu.VMEM((padded, cap6), F32),
            pltpu.VMEM((padded // 8, 8 * cap5), F32),
            pltpu.VMEM((padded // 8, 8 * cap5), F32),
            pltpu.VMEM((padded // STEP, STEP * cap4), F32),
            pltpu.VMEM((padded // STEP, STEP * cap4), F32),
            pltpu.VMEM((boxes, padded * cap6), BF16),
            pltpu.VMEM((boxes, padded * cap6), BF16),
            pltpu.VMEM((STEP // 2, 2 * width, 2 * cap6), BF16),
            pltpu.VMEM((rows, padded * width), BF16),
            pltpu.VMEM((n_s, quarter + PACK, width), BF16),
            pltpu.VMEM((n_s, quarter + PACK, width), BF16),
            pltpu.VMEM((slots * PACK, slots * 8), BF16),
            pltpu.VMEM((slots * PACK, slots), BF16),
            sems((13,)),
            sems((2 + n_s,)),
            sems((3 * n_s,)),
            sems((2 * n_s,)),
            sems((n_s,)),
            sems((n_s,)),
            sems((GROUP,)),
            sems((GROUP,)),
            sems((n_s,)),
            sems((n_s,)),
        ],
        compiler_params=pltpu.CompilerParams(
            collective_id=0, has_side_effects=True, vmem_limit_bytes=63 * 1024 * 1024
        ),
        name="far_field",
    )(mult, trans, up, down, t6, s6, c6, t5, s5, c5, t4, s4, c4)


def solution(mesh):
    sizes = (mesh.shape["morton"], mesh.shape["sub"])
    placed = (
        P(("morton", "sub"), None),
        P("sub", None, None),
        P(),
        P(),
        P("morton", "sub", None),
        P("morton", "sub", None),
        P("morton", "sub"),
        P("morton", "sub", None),
        P("morton", "sub", None),
        P("morton", "sub"),
        P("morton", "sub", None),
        P("morton", "sub", None),
        P("morton", "sub"),
    )
    return jax.shard_map(
        functools.partial(local, sizes),
        mesh=mesh,
        in_specs=placed,
        out_specs=P(("morton", "sub"), None),
        check_vma=False,
    )
```

```python
import functools

import jax
import jax.numpy as jnp
from jax import lax
from jax.experimental import pallas as pl
from jax.experimental.pallas import tpu as pltpu
from jax.sharding import PartitionSpec as P

BF16 = jnp.bfloat16
F32 = jnp.float32
MESH = pl.DeviceIdType.MESH
GROUP = 8
PACK = 16
STEP = 16


def dot(a, b):
    return jnp.dot(a, b, preferred_element_type=F32)


def dot_nt(a, b):
    return lax.dot_general(a, b, (((1,), (1,)), ((), ())), preferred_element_type=F32)


def column_of(row, height):
    width = row.shape[1]
    at = lax.broadcasted_iota(jnp.int32, (height, width), 0)
    on = lax.broadcasted_iota(jnp.int32, (height, width), 1)
    return jnp.sum(jnp.where(at == on, row, 0.0), axis=1, keepdims=True)


def folded(values, per_row):
    n, cap = values.shape
    lanes = per_row * cap
    j = lax.broadcasted_iota(jnp.int32, (cap, lanes), 0)
    lane = lax.broadcasted_iota(jnp.int32, (cap, lanes), 1)
    spread = jnp.where(lane % cap == j, 1.0, 0.0).astype(BF16)
    wide = dot(values.astype(BF16), spread)
    at = lax.broadcasted_iota(jnp.int32, (n, lanes), 0)
    on = lax.broadcasted_iota(jnp.int32, (n, lanes), 1)
    wide = jnp.where(at % per_row == on // cap, wide, 0.0).astype(BF16)
    out = lax.broadcasted_iota(jnp.int32, (n // per_row, n), 0)
    src = lax.broadcasted_iota(jnp.int32, (n // per_row, n), 1)
    return dot(jnp.where(src // per_row == out, 1.0, 0.0).astype(BF16), wide)


def one_hot(ids, row):
    height, lanes = ids.shape
    rows = jnp.broadcast_to(row, (16, lanes)).astype(BF16)
    same = ids.reshape(height // 16, 16, lanes) == rows[None]
    one, none = jnp.ones((), BF16), jnp.zeros((), BF16)
    return jnp.where(same, one, none).reshape(height, lanes)


def wrapped(value, size):
    return jnp.where(value >= size, value - size, value)


def upward_rows(children, up, wide):
    parents = children.shape[0] // 8
    wide[...] = children.astype(F32)
    rows = [wide[pl.ds(c, parents, stride=8), :] for c in range(8)]
    ops = up.reshape(-1, up.shape[2])
    five = dot(jnp.concatenate(rows, axis=1).astype(BF16), ops).astype(BF16).astype(F32)
    row = jnp.concatenate([five[c : c + 1, :] for c in range(8)], axis=1).astype(BF16)
    pad = jnp.zeros((PACK - parents - 1, five.shape[1]), F32)
    return jnp.concatenate([five, dot(row, ops), pad], axis=0).astype(BF16)


def kernel(
    sizes, mult_hbm, tr_hbm, up_hbm, down_hbm, t6_hbm, s6_hbm, c6_hbm, t5_hbm, s5_hbm, c5_hbm,
    t4_hbm, s4_hbm, c4_hbm, out_ref,
    near, coarse, mats, up, down, t6, s6, c6, t5, s5, c5, t4, s4, c4,
    wide, mt, c5t, c4t, tg6, sr6, bl6, tg5, sr5, tg4, sr4,
    picks, places, apart, gather, turned, products, parts, got, choose5,
    choose4,
    load, near_send, near_recv, pass_send, pack_send, pack_recv, join_send, join_recv,
    part_send, part_recv,
):
    n_m, n_s = sizes
    n_ops, width = tr_hbm.shape[0], tr_hbm.shape[2]
    padded = mats.shape[0]
    quarter = near.shape[1]
    boxes = quarter * n_s
    fives, fours = boxes // 8, boxes // 64
    cap6, cap5, cap4 = t6.shape[2], t5.shape[1], t4.shape[1]
    m, s = lax.axis_index("morton"), lax.axis_index("sub")
    base = m * 0 if n_m == GROUP else m // GROUP * GROUP
    here = m - base
    following = wrapped(m + 1, n_m)
    previous = jnp.where(m == 0, n_m - 1, m - 1)

    barrier = pltpu.get_barrier_semaphore()

    def greet(peer):
        pl.semaphore_signal(barrier, inc=1, device_id=peer, device_id_type=MESH)

    for k in range(1, n_s):
        greet((m, wrapped(s + k, n_s)))
    for k in range(1, GROUP):
        greet((base + wrapped(here + k, GROUP), s))
    expected = n_s - 1 + GROUP - 1
    if n_m > GROUP:
        greet((following, s))
        greet((previous, s))
        expected = expected + 2

    own = near.at[n_s + s]
    pairs = [
        (mult_hbm, own), (up_hbm, up), (c6_hbm, c6), (t6_hbm, t6), (s6_hbm, s6),
        (c5_hbm, c5), (t5_hbm, t5), (s5_hbm, s5), (c4_hbm, c4), (t4_hbm, t4), (s4_hbm, s4),
        (tr_hbm, mats.at[pl.ds(0, n_ops)]), (down_hbm, down),
    ]
    loads = [pltpu.make_async_copy(a, b, load.at[i]) for i, (a, b) in enumerate(pairs)]
    for copy in loads:
        copy.start()

    def remote(src, dst, send, recv, peer):
        return pltpu.make_async_remote_copy(
            src_ref=src, dst_ref=dst, send_sem=send, recv_sem=recv,
            device_id=peer, device_id_type=MESH,
        )

    def halo_copy(side):
        slot = side * 2 * n_s + s
        return remote(
            own, near.at[slot], near_send.at[side], near_recv.at[slot],
            (previous if side else following, s),
        )

    def sub_copy(k, there):
        other = wrapped(s + k, n_s)
        slot = n_s + (other if there else s)
        return remote(
            own, near.at[slot], near_send.at[2 + k], near_recv.at[slot], (m, other)
        )

    def pass_copy(side, k, there):
        other = wrapped(s + k, n_s)
        slot = side * 2 * n_s + (other if there else s)
        return remote(
            near.at[slot], near.at[slot], pass_send.at[side * n_s + k], near_recv.at[slot],
            (m, other),
        )

    def pack_copy(k, there):
        other = wrapped(s + k, n_s)
        slot = coarse.at[here, other if there else s]
        return remote(
            slot, slot, pack_send.at[k], pack_recv.at[other if there else s], (m, other)
        )

    def join_copy(k, there):
        other = wrapped(here + k, GROUP)
        slot = other if there else here
        return remote(
            coarse.at[slot], coarse.at[slot], join_send.at[k], join_recv.at[slot],
            (base + other, s),
        )

    def part_copy(k):
        other = wrapped(s + k, n_s)
        return remote(
            parts.at[other], got.at[k], part_send.at[k], part_recv.at[k], (m, other)
        )

    loads[0].wait()
    pl.semaphore_wait(barrier, expected)
    for side in range(2):
        halo_copy(side).start()
    for k in range(1, n_s):
        sub_copy(k, False).start()
    loads[1].wait()
    coarse[here, s] = upward_rows(near[n_s + s], up[...], wide)
    for k in range(1, n_s):
        pack_copy(k, False).start()

    for copy in loads[2:11]:
        copy.wait()

    def filled(values, fill):
        if padded == n_ops:
            return values
        more = jnp.full((padded - n_ops, values.shape[1]), fill, F32)
        return jnp.concatenate([values, more], axis=0)

    lane = lax.broadcasted_iota(jnp.int32, (n_ops, cap6), 1).astype(F32)
    live = lane < column_of(c6[...].astype(F32), n_ops)
    tg6[...] = filled(jnp.where(live, t6[:, 0, :].astype(F32), -1.0), -1.0)
    source = s6[:, 0, :]
    block = jnp.where(source >= boxes, 1, 0) + jnp.where(source >= 2 * boxes, 1, 0)
    sr6[...] = filled((source - block * boxes).astype(F32), 0.0)
    bl6[...] = filled(block.astype(F32), 0.0)

    at = lax.broadcasted_iota(jnp.int32, (padded, n_ops), 0)
    on = lax.broadcasted_iota(jnp.int32, (padded, n_ops), 1)
    turn = jnp.where(at == on, 1.0, 0.0).astype(BF16)

    def keys(t_ref, c_ref, per_row, height):
        cap = t_ref.shape[1]
        slot = lax.broadcasted_iota(jnp.int32, (cap, n_ops), 0)
        alive = jnp.where(slot < c_ref[...], t_ref[0] + 1, 0).astype(F32).astype(BF16)
        raw = folded(dot_nt(turn, alive), per_row)
        lane = lax.broadcasted_iota(jnp.int32, raw.shape, 1) // cap
        return jnp.where(raw > 0.0, raw - 1.0 + (lane * height).astype(F32), -1.0)

    def sources(s_ref, per_row):
        return folded(dot_nt(turn, s_ref[0].astype(F32).astype(BF16)), per_row)

    tg5[...] = keys(t5, c5, 8, fives)
    sr5[...] = sources(s5, 8)
    tg4[...] = keys(t4, c4, STEP, PACK)
    sr4[...] = sources(s4, STEP)

    for side in range(2):
        halo_copy(side).wait_recv()
        for k in range(1, n_s):
            pass_copy(side, k, False).start()
    for k in range(1, n_s):
        pack_copy(k, True).wait_recv()
    for k in range(1, GROUP):
        join_copy(k, False).start()
    slots = GROUP * n_s
    q = lax.broadcasted_iota(jnp.int32, (slots * PACK, slots * 8), 0)
    p = lax.broadcasted_iota(jnp.int32, (slots * PACK, slots * 8), 1)
    choose5[...] = jnp.where(q == p // 8 * PACK + p % 8, 1.0, 0.0).astype(BF16)
    q = lax.broadcasted_iota(jnp.int32, (slots * PACK, slots), 0)
    p = lax.broadcasted_iota(jnp.int32, (slots * PACK, slots), 1)
    choose4[...] = jnp.where(q == p * PACK + 8, 1.0, 0.0).astype(BF16)

    apart[...] = jnp.zeros(apart.shape, BF16)
    for o in range(n_ops, padded):
        mats[o] = jnp.zeros(mats.shape[1:], BF16)
    ids = lax.broadcasted_iota(jnp.int32, (boxes, cap6), 0).astype(F32).astype(BF16)

    @pl.loop(0, padded // STEP)
    def _(step):
        for j in range(STEP):
            lanes = pl.ds(pl.multiple_of(step * STEP * cap6 + j * cap6, cap6), cap6)
            picks[:, lanes] = one_hot(ids, sr6[pl.ds(step * STEP + j, 1), :])
            places[:, lanes] = one_hot(ids, tg6[pl.ds(step * STEP + j, 1), :])

    r = lax.broadcasted_iota(jnp.int32, (width, width), 0)
    c = lax.broadcasted_iota(jnp.int32, (width, width), 1)
    eye = jnp.where(r == c, 1.0, 0.0).astype(BF16)

    loads[11].wait()

    @pl.loop(0, padded // STEP)
    def _(step):
        for pair in range(STEP // 2):
            both = mats[pl.ds(step * STEP + 2 * pair, 2)].reshape(2 * width, width)
            start = step * STEP * width + 2 * pair * width
            lanes = pl.ds(pl.multiple_of(start, 2 * width), 2 * width)
            turned[:, lanes] = dot_nt(eye, both).astype(BF16)

    for k in range(1, n_s):
        sub_copy(k, True).wait_recv()
    for side in range(2):
        for k in range(1, n_s):
            pass_copy(side, k, True).wait_recv()

    nearby = near[...].reshape(3, boxes, width)
    for block in range(3):
        rows = dot_nt(eye, nearby[block])
        if block == 0:
            rows = jnp.where(m == 0, 0.0, rows)
        if block == 2:
            rows = jnp.where(m == n_m - 1, 0.0, rows)
        mt[pl.ds(block * width, width), :] = rows.astype(BF16)

    quads = STEP // 4

    @pl.loop(0, padded // STEP)
    def _(step):
        def pick(quad):
            start = step * STEP * cap6 + 4 * quad * cap6
            lanes = pl.ds(pl.multiple_of(start, 4 * cap6), 4 * cap6)
            found = dot(mt[...], picks[:, lanes]).astype(BF16)
            for k in range(4):
                o = 4 * quad + k
                head = bl6[pl.ds(step * STEP + o, 1), :]
                head = jnp.broadcast_to(head, (16, cap6)).astype(BF16)[None]
                piece = found[:, k * cap6 : (k + 1) * cap6].reshape(3, width // 16, 16, cap6)
                chosen = jnp.where(head == 1.0, piece[1], piece[2])
                chosen = jnp.where(head == 0.0, piece[0], chosen)
                half = o % 2
                apart[o // 2, pl.ds(half * width, width), pl.ds(half * cap6, cap6)] = (
                    chosen.reshape(width, cap6)
                )

        def translate(pair):
            start = step * STEP * width + 2 * pair * width
            lanes = pl.ds(pl.multiple_of(start, 2 * width), 2 * width)
            start = step * STEP * cap6 + 2 * pair * cap6
            slots = pl.ds(pl.multiple_of(start, 2 * cap6), 2 * cap6)
            products[:, slots] = dot(turned[:, lanes], apart[pair]).astype(BF16)

        for turn in range(quads + 1):
            if turn >= 1:
                translate(2 * turn - 2)
                translate(2 * turn - 1)
            if turn < quads:
                pick(turn)

    for k in range(1, GROUP):
        join_copy(k, True).wait_recv()
    packed = dot_nt(eye, coarse[...].reshape(slots * PACK, width)).astype(BF16)
    c5t[...] = dot(packed, choose5[...]).astype(BF16)
    c4t[...] = dot(packed, choose4[...]).astype(BF16)

    def numbers(height, lanes):
        return lax.broadcasted_iota(jnp.int32, (height, lanes), 0).astype(F32).astype(BF16)

    source5, target5 = numbers(slots * 8, 8 * cap5), numbers(8 * fives, 8 * cap5)
    source4, target4 = numbers(slots, STEP * cap4), numbers(STEP * PACK, STEP * cap4)

    for step in range(padded // STEP):

        def at(o, step=step):
            return pl.ds((step * STEP + o) * width, width)

        for half in range(STEP // 8):
            row = step * (STEP // 8) + half
            found = dot(c5t[...], one_hot(source5, sr5[pl.ds(row, 1), :])).astype(BF16)
            placed = dot_nt(one_hot(target5, tg5[pl.ds(row, 1), :]), found).astype(BF16)
            for o in range(8):
                gather[pl.ds(0, fives), at(half * 8 + o)] = placed[o * fives : (o + 1) * fives]
        found = dot(c4t[...], one_hot(source4, sr4[pl.ds(step, 1), :])).astype(BF16)
        placed = dot_nt(one_hot(target4, tg4[pl.ds(step, 1), :]), found).astype(BF16)
        for o in range(STEP):
            gather[pl.ds(fives, PACK), at(o)] = placed[o * PACK : (o + 1) * PACK]

    total = dot_nt(products[...], places[...]).T
    low = dot(gather[...], mats[...].reshape(padded * width, width))

    six, five, four = boxes // n_s, fives // n_s, fours // n_s
    for part in range(n_s):
        parts[part, pl.ds(0, six), :] = total[part * six : (part + 1) * six].astype(BF16)
        last = fives + part * four
        tail = jnp.concatenate(
            [
                low[part * five : (part + 1) * five] * 0.5,
                low[last : last + four] * 0.25,
                jnp.zeros((PACK - five - four, width), F32),
            ],
            axis=0,
        )
        parts[part, pl.ds(six, PACK), :] = tail.astype(BF16)
    for k in range(1, n_s):
        part_copy(k).start()
    loads[12].wait()
    whole = parts[s].astype(F32)
    for k in range(1, n_s):
        part_copy(k).wait_recv()
        whole = whole + got[k].astype(F32)
    row = whole[six + five : six + five + 1, :].astype(BF16)
    spread = [dot(row, down[c]) for c in range(8)]
    mid = (whole[six : six + five, :] + jnp.concatenate(spread, axis=0)).astype(BF16)
    for c in range(8):
        wide[pl.ds(c, six // 8, stride=8), :] = dot(mid, down[c])
    out_ref[...] = (wide[...] + whole[:six, :]).astype(BF16)

    for side in range(2):
        halo_copy(side).wait_send()
        for k in range(1, n_s):
            pass_copy(side, k, False).wait_send()
    for k in range(1, n_s):
        sub_copy(k, False).wait_send()
        pack_copy(k, False).wait_send()
        part_copy(k).wait_send()
    for k in range(1, GROUP):
        join_copy(k, False).wait_send()


def local(sizes, mult, trans, up, down, t6, s6, c6, t5, s5, c5, t4, s4, c4):
    n_m, n_s = sizes
    quarter, width = mult.shape
    boxes = quarter * n_s
    slots = GROUP * n_s
    n_ops = trans.shape[0]
    padded = -(-n_ops // STEP) * STEP
    rows = boxes // 8 + PACK
    cap6, cap5, cap4 = t6.shape[2], t5.shape[2], t4.shape[2]
    t6, s6 = jnp.swapaxes(t6, 0, 1), jnp.swapaxes(s6, 0, 1)
    t5, s5, t4, s4 = (jnp.swapaxes(x, 1, 2) for x in (t5, s5, t4, s4))
    index = [pltpu.VMEM(x.shape, x.dtype) for x in (t6, s6, c6, t5, s5, c5, t4, s4, c4)]
    sems = pltpu.SemaphoreType.DMA
    return pl.pallas_call(
        functools.partial(kernel, sizes),
        out_shape=jax.ShapeDtypeStruct((quarter, width), BF16),
        in_specs=[pl.BlockSpec(memory_space=pltpu.HBM)] * 13,
        out_specs=pl.BlockSpec(memory_space=pltpu.VMEM),
        scratch_shapes=[
            pltpu.VMEM((3 * n_s, quarter, width), BF16),
            pltpu.VMEM((GROUP, n_s, PACK, width), BF16),
            pltpu.VMEM((padded, width, width), BF16),
            pltpu.VMEM(up.shape, BF16),
            pltpu.VMEM(down.shape, BF16),
            *index,
            pltpu.VMEM((quarter, width), F32),
            pltpu.VMEM((3 * width, boxes), BF16),
            pltpu.VMEM((width, slots * 8), BF16),
            pltpu.VMEM((width, slots), BF16),
            pltpu.VMEM((padded, cap6), F32),
            pltpu.VMEM((padded, cap6), F32),
            pltpu.VMEM((padded, cap6), F32),
            pltpu.VMEM((padded // 8, 8 * cap5), F32),
            pltpu.VMEM((padded // 8, 8 * cap5), F32),
            pltpu.VMEM((padded // STEP, STEP * cap4), F32),
            pltpu.VMEM((padded // STEP, STEP * cap4), F32),
            pltpu.VMEM((boxes, padded * cap6), BF16),
            pltpu.VMEM((boxes, padded * cap6), BF16),
            pltpu.VMEM((STEP // 2, 2 * width, 2 * cap6), BF16),
            pltpu.VMEM((rows, padded * width), BF16),
            pltpu.VMEM((width, padded * width), BF16),
            pltpu.VMEM((width, padded * cap6), BF16),
            pltpu.VMEM((n_s, quarter + PACK, width), BF16),
            pltpu.VMEM((n_s, quarter + PACK, width), BF16),
            pltpu.VMEM((slots * PACK, slots * 8), BF16),
            pltpu.VMEM((slots * PACK, slots), BF16),
            sems((13,)),
            sems((2 + n_s,)),
            sems((3 * n_s,)),
            sems((2 * n_s,)),
            sems((n_s,)),
            sems((n_s,)),
            sems((GROUP,)),
            sems((GROUP,)),
            sems((n_s,)),
            sems((n_s,)),
        ],
        compiler_params=pltpu.CompilerParams(
            collective_id=0, has_side_effects=True, vmem_limit_bytes=63 * 1024 * 1024
        ),
        name="far_field",
    )(mult, trans, up, down, t6, s6, c6, t5, s5, c5, t4, s4, c4)


def solution(mesh):
    sizes = (mesh.shape["morton"], mesh.shape["sub"])
    placed = (
        P(("morton", "sub"), None),
        P("sub", None, None),
        P(),
        P(),
        P("morton", "sub", None),
        P("morton", "sub", None),
        P("morton", "sub"),
        P("morton", "sub", None),
        P("morton", "sub", None),
        P("morton", "sub"),
        P("morton", "sub", None),
        P("morton", "sub", None),
        P("morton", "sub"),
    )
    return jax.shard_map(
        functools.partial(local, sizes),
        mesh=mesh,
        in_specs=placed,
        out_specs=P(("morton", "sub"), None),
        check_vma=False,
    )
```

```python
import functools

import jax
import jax.numpy as jnp
from jax import lax
from jax.experimental import pallas as pl
from jax.experimental.pallas import tpu as pltpu
from jax.sharding import PartitionSpec as P

BF16 = jnp.bfloat16
F32 = jnp.float32
MESH = pl.DeviceIdType.MESH
GROUP = 8
PACK = 16
STEP = 16


def dot(a, b):
    return jnp.dot(a, b, preferred_element_type=F32)


def dot_nt(a, b):
    return lax.dot_general(a, b, (((1,), (1,)), ((), ())), preferred_element_type=F32)


def column_of(row, height):
    width = row.shape[1]
    at = lax.broadcasted_iota(jnp.int32, (height, width), 0)
    on = lax.broadcasted_iota(jnp.int32, (height, width), 1)
    return jnp.sum(jnp.where(at == on, row, 0.0), axis=1, keepdims=True)


def folded(values, per_row):
    n, cap = values.shape
    lanes = per_row * cap
    j = lax.broadcasted_iota(jnp.int32, (cap, lanes), 0)
    lane = lax.broadcasted_iota(jnp.int32, (cap, lanes), 1)
    spread = jnp.where(lane % cap == j, 1.0, 0.0).astype(BF16)
    wide = dot(values.astype(BF16), spread)
    at = lax.broadcasted_iota(jnp.int32, (n, lanes), 0)
    on = lax.broadcasted_iota(jnp.int32, (n, lanes), 1)
    wide = jnp.where(at % per_row == on // cap, wide, 0.0).astype(BF16)
    out = lax.broadcasted_iota(jnp.int32, (n // per_row, n), 0)
    src = lax.broadcasted_iota(jnp.int32, (n // per_row, n), 1)
    return dot(jnp.where(src // per_row == out, 1.0, 0.0).astype(BF16), wide)


def one_hot(ids, row):
    height, lanes = ids.shape
    rows = jnp.broadcast_to(row, (16, lanes)).astype(BF16)
    same = ids.reshape(height // 16, 16, lanes) == rows[None]
    one, none = jnp.ones((), BF16), jnp.zeros((), BF16)
    return jnp.where(same, one, none).reshape(height, lanes)


def wrapped(value, size):
    return jnp.where(value >= size, value - size, value)


def upward_rows(children, up, wide):
    parents = children.shape[0] // 8
    wide[...] = children.astype(F32)
    rows = [wide[pl.ds(c, parents, stride=8), :] for c in range(8)]
    ops = up.reshape(-1, up.shape[2])
    five = dot(jnp.concatenate(rows, axis=1).astype(BF16), ops).astype(BF16).astype(F32)
    row = jnp.concatenate([five[c : c + 1, :] for c in range(8)], axis=1).astype(BF16)
    pad = jnp.zeros((PACK - parents - 1, five.shape[1]), F32)
    return jnp.concatenate([five, dot(row, ops), pad], axis=0).astype(BF16)


def kernel(
    sizes, mult_hbm, tr_hbm, up_hbm, down_hbm, t6_hbm, s6_hbm, c6_hbm, t5_hbm, s5_hbm, c5_hbm,
    t4_hbm, s4_hbm, c4_hbm, out_ref,
    near, coarse, mats, up, down, t6, s6, c6, t5, s5, c5, t4, s4, c4,
    wide, mt, c5t, c4t, tg6, sr6, bl6, tg5, sr5, tg4, sr4,
    picks, places, apart, gather, turned, products, parts, got, choose5,
    choose4,
    load, near_send, near_recv, pass_send, pack_send, pack_recv, join_send, join_recv,
    part_send, part_recv,
):
    n_m, n_s = sizes
    n_ops, width = tr_hbm.shape[0], tr_hbm.shape[2]
    padded = mats.shape[0]
    quarter = near.shape[1]
    boxes = quarter * n_s
    fives, fours = boxes // 8, boxes // 64
    cap6, cap5, cap4 = t6.shape[2], t5.shape[1], t4.shape[1]
    m, s = lax.axis_index("morton"), lax.axis_index("sub")
    base = m * 0 if n_m == GROUP else m // GROUP * GROUP
    here = m - base
    following = wrapped(m + 1, n_m)
    previous = jnp.where(m == 0, n_m - 1, m - 1)

    barrier = pltpu.get_barrier_semaphore()

    def greet(peer):
        pl.semaphore_signal(barrier, inc=1, device_id=peer, device_id_type=MESH)

    for k in range(1, n_s):
        greet((m, wrapped(s + k, n_s)))
    for k in range(1, GROUP):
        greet((base + wrapped(here + k, GROUP), s))
    expected = n_s - 1 + GROUP - 1
    if n_m > GROUP:
        greet((following, s))
        greet((previous, s))
        expected = expected + 2

    own = near.at[n_s + s]
    pairs = [
        (mult_hbm, own), (up_hbm, up), (c6_hbm, c6), (t6_hbm, t6), (s6_hbm, s6),
        (c5_hbm, c5), (t5_hbm, t5), (s5_hbm, s5), (c4_hbm, c4), (t4_hbm, t4), (s4_hbm, s4),
        (tr_hbm, mats.at[pl.ds(0, n_ops)]), (down_hbm, down),
    ]
    loads = [pltpu.make_async_copy(a, b, load.at[i]) for i, (a, b) in enumerate(pairs)]
    for copy in loads:
        copy.start()

    def remote(src, dst, send, recv, peer):
        return pltpu.make_async_remote_copy(
            src_ref=src, dst_ref=dst, send_sem=send, recv_sem=recv,
            device_id=peer, device_id_type=MESH,
        )

    def halo_copy(side):
        slot = side * 2 * n_s + s
        return remote(
            own, near.at[slot], near_send.at[side], near_recv.at[slot],
            (previous if side else following, s),
        )

    def sub_copy(k, there):
        other = wrapped(s + k, n_s)
        slot = n_s + (other if there else s)
        return remote(
            own, near.at[slot], near_send.at[2 + k], near_recv.at[slot], (m, other)
        )

    def pass_copy(side, k, there):
        other = wrapped(s + k, n_s)
        slot = side * 2 * n_s + (other if there else s)
        return remote(
            near.at[slot], near.at[slot], pass_send.at[side * n_s + k], near_recv.at[slot],
            (m, other),
        )

    def pack_copy(k, there):
        other = wrapped(s + k, n_s)
        slot = coarse.at[here, other if there else s]
        return remote(
            slot, slot, pack_send.at[k], pack_recv.at[other if there else s], (m, other)
        )

    def join_copy(k, there):
        other = wrapped(here + k, GROUP)
        slot = other if there else here
        return remote(
            coarse.at[slot], coarse.at[slot], join_send.at[k], join_recv.at[slot],
            (base + other, s),
        )

    def part_copy(k):
        other = wrapped(s + k, n_s)
        return remote(
            parts.at[other], got.at[k], part_send.at[k], part_recv.at[k], (m, other)
        )

    loads[0].wait()
    pl.semaphore_wait(barrier, expected)
    for side in range(2):
        halo_copy(side).start()
    for k in range(1, n_s):
        sub_copy(k, False).start()
    loads[1].wait()
    coarse[here, s] = upward_rows(near[n_s + s], up[...], wide)
    for k in range(1, n_s):
        pack_copy(k, False).start()

    for copy in loads[2:11]:
        copy.wait()

    def filled(values, fill):
        if padded == n_ops:
            return values
        more = jnp.full((padded - n_ops, values.shape[1]), fill, F32)
        return jnp.concatenate([values, more], axis=0)

    lane = lax.broadcasted_iota(jnp.int32, (n_ops, cap6), 1).astype(F32)
    live = lane < column_of(c6[...].astype(F32), n_ops)
    tg6[...] = filled(jnp.where(live, t6[:, 0, :].astype(F32), -1.0), -1.0)
    source = s6[:, 0, :]
    block = jnp.where(source >= boxes, 1, 0) + jnp.where(source >= 2 * boxes, 1, 0)
    sr6[...] = filled((source - block * boxes).astype(F32), 0.0)
    bl6[...] = filled(block.astype(F32), 0.0)

    at = lax.broadcasted_iota(jnp.int32, (padded, n_ops), 0)
    on = lax.broadcasted_iota(jnp.int32, (padded, n_ops), 1)
    turn = jnp.where(at == on, 1.0, 0.0).astype(BF16)

    def keys(t_ref, c_ref, per_row, height):
        cap = t_ref.shape[1]
        slot = lax.broadcasted_iota(jnp.int32, (cap, n_ops), 0)
        alive = jnp.where(slot < c_ref[...], t_ref[0] + 1, 0).astype(F32).astype(BF16)
        raw = folded(dot_nt(turn, alive), per_row)
        lane = lax.broadcasted_iota(jnp.int32, raw.shape, 1) // cap
        return jnp.where(raw > 0.0, raw - 1.0 + (lane * height).astype(F32), -1.0)

    def sources(s_ref, per_row):
        return folded(dot_nt(turn, s_ref[0].astype(F32).astype(BF16)), per_row)

    tg5[...] = keys(t5, c5, 8, fives)
    sr5[...] = sources(s5, 8)
    tg4[...] = keys(t4, c4, STEP, PACK)
    sr4[...] = sources(s4, STEP)

    for side in range(2):
        halo_copy(side).wait_recv()
        for k in range(1, n_s):
            pass_copy(side, k, False).start()
    for k in range(1, n_s):
        pack_copy(k, True).wait_recv()
    for k in range(1, GROUP):
        join_copy(k, False).start()
    slots = GROUP * n_s
    q = lax.broadcasted_iota(jnp.int32, (slots * PACK, slots * 8), 0)
    p = lax.broadcasted_iota(jnp.int32, (slots * PACK, slots * 8), 1)
    choose5[...] = jnp.where(q == p // 8 * PACK + p % 8, 1.0, 0.0).astype(BF16)
    q = lax.broadcasted_iota(jnp.int32, (slots * PACK, slots), 0)
    p = lax.broadcasted_iota(jnp.int32, (slots * PACK, slots), 1)
    choose4[...] = jnp.where(q == p * PACK + 8, 1.0, 0.0).astype(BF16)

    apart[...] = jnp.zeros(apart.shape, BF16)
    for o in range(n_ops, padded):
        mats[o] = jnp.zeros(mats.shape[1:], BF16)
    ids = lax.broadcasted_iota(jnp.int32, (boxes, cap6), 0).astype(F32).astype(BF16)

    @pl.loop(0, padded // STEP)
    def _(step):
        for j in range(STEP):
            lanes = pl.ds(pl.multiple_of(step * STEP * cap6 + j * cap6, cap6), cap6)
            picks[:, lanes] = one_hot(ids, sr6[pl.ds(step * STEP + j, 1), :])

    r = lax.broadcasted_iota(jnp.int32, (width, width), 0)
    c = lax.broadcasted_iota(jnp.int32, (width, width), 1)
    eye = jnp.where(r == c, 1.0, 0.0).astype(BF16)

    loads[11].wait()

    @pl.loop(0, padded // STEP)
    def _(step):
        for pair in range(STEP // 2):
            both = mats[pl.ds(step * STEP + 2 * pair, 2)].reshape(2 * width, width)
            start = step * STEP * width + 2 * pair * width
            lanes = pl.ds(pl.multiple_of(start, 2 * width), 2 * width)
            turned[:, lanes] = dot_nt(eye, both).astype(BF16)

    for k in range(1, n_s):
        sub_copy(k, True).wait_recv()
    for side in range(2):
        for k in range(1, n_s):
            pass_copy(side, k, True).wait_recv()

    nearby = near[...].reshape(3, boxes, width)
    for block in range(3):
        rows = dot_nt(eye, nearby[block])
        if block == 0:
            rows = jnp.where(m == 0, 0.0, rows)
        if block == 2:
            rows = jnp.where(m == n_m - 1, 0.0, rows)
        mt[pl.ds(block * width, width), :] = rows.astype(BF16)

    quads = STEP // 4

    @pl.loop(0, padded // STEP)
    def _(step):
        def pick(quad):
            start = step * STEP * cap6 + 4 * quad * cap6
            lanes = pl.ds(pl.multiple_of(start, 4 * cap6), 4 * cap6)
            found = dot(mt[...], picks[:, lanes]).astype(BF16)
            for k in range(4):
                o = 4 * quad + k
                head = bl6[pl.ds(step * STEP + o, 1), :]
                head = jnp.broadcast_to(head, (16, cap6)).astype(BF16)[None]
                piece = found[:, k * cap6 : (k + 1) * cap6].reshape(3, width // 16, 16, cap6)
                chosen = jnp.where(head == 1.0, piece[1], piece[2])
                chosen = jnp.where(head == 0.0, piece[0], chosen)
                half = o % 2
                apart[o // 2, pl.ds(half * width, width), pl.ds(half * cap6, cap6)] = (
                    chosen.reshape(width, cap6)
                )
                lanes = pl.ds(pl.multiple_of((step * STEP + o) * cap6, cap6), cap6)
                places[:, lanes] = one_hot(ids, tg6[pl.ds(step * STEP + o, 1), :])

        def translate(pair):
            start = step * STEP * width + 2 * pair * width
            lanes = pl.ds(pl.multiple_of(start, 2 * width), 2 * width)
            start = step * STEP * cap6 + 2 * pair * cap6
            slots = pl.ds(pl.multiple_of(start, 2 * cap6), 2 * cap6)
            products[:, slots] = dot(turned[:, lanes], apart[pair]).astype(BF16)

        for turn in range(quads + 1):
            if turn >= 1:
                translate(2 * turn - 2)
                translate(2 * turn - 1)
            if turn < quads:
                pick(turn)

    for k in range(1, GROUP):
        join_copy(k, True).wait_recv()
    packed = dot_nt(eye, coarse[...].reshape(slots * PACK, width)).astype(BF16)
    c5t[...] = dot(packed, choose5[...]).astype(BF16)
    c4t[...] = dot(packed, choose4[...]).astype(BF16)

    def numbers(height, lanes):
        return lax.broadcasted_iota(jnp.int32, (height, lanes), 0).astype(F32).astype(BF16)

    source5, target5 = numbers(slots * 8, 8 * cap5), numbers(8 * fives, 8 * cap5)
    source4, target4 = numbers(slots, STEP * cap4), numbers(STEP * PACK, STEP * cap4)

    for step in range(padded // STEP):

        def at(o, step=step):
            return pl.ds((step * STEP + o) * width, width)

        for half in range(STEP // 8):
            row = step * (STEP // 8) + half
            found = dot(c5t[...], one_hot(source5, sr5[pl.ds(row, 1), :])).astype(BF16)
            placed = dot_nt(one_hot(target5, tg5[pl.ds(row, 1), :]), found).astype(BF16)
            for o in range(8):
                gather[pl.ds(0, fives), at(half * 8 + o)] = placed[o * fives : (o + 1) * fives]
        found = dot(c4t[...], one_hot(source4, sr4[pl.ds(step, 1), :])).astype(BF16)
        placed = dot_nt(one_hot(target4, tg4[pl.ds(step, 1), :]), found).astype(BF16)
        for o in range(STEP):
            gather[pl.ds(fives, PACK), at(o)] = placed[o * PACK : (o + 1) * PACK]

    total, low = 0.0, 0.0
    for step in range(padded // STEP):
        lanes = pl.ds(step * STEP * cap6, STEP * cap6)
        total = total + dot_nt(products[:, lanes], places[:, lanes])
        ops = mats[pl.ds(step * STEP, STEP)].reshape(STEP * width, width)
        low = low + dot(gather[:, pl.ds(step * STEP * width, STEP * width)], ops)
    total = total.T

    six, five, four = boxes // n_s, fives // n_s, fours // n_s
    for part in range(n_s):
        parts[part, pl.ds(0, six), :] = total[part * six : (part + 1) * six].astype(BF16)
        last = fives + part * four
        tail = jnp.concatenate(
            [
                low[part * five : (part + 1) * five] * 0.5,
                low[last : last + four] * 0.25,
                jnp.zeros((PACK - five - four, width), F32),
            ],
            axis=0,
        )
        parts[part, pl.ds(six, PACK), :] = tail.astype(BF16)
    for k in range(1, n_s):
        part_copy(k).start()
    loads[12].wait()
    whole = parts[s].astype(F32)
    for k in range(1, n_s):
        part_copy(k).wait_recv()
        whole = whole + got[k].astype(F32)
    row = whole[six + five : six + five + 1, :].astype(BF16)
    spread = [dot(row, down[c]) for c in range(8)]
    mid = (whole[six : six + five, :] + jnp.concatenate(spread, axis=0)).astype(BF16)
    for c in range(8):
        wide[pl.ds(c, six // 8, stride=8), :] = dot(mid, down[c])
    out_ref[...] = (wide[...] + whole[:six, :]).astype(BF16)

    for side in range(2):
        halo_copy(side).wait_send()
        for k in range(1, n_s):
            pass_copy(side, k, False).wait_send()
    for k in range(1, n_s):
        sub_copy(k, False).wait_send()
        pack_copy(k, False).wait_send()
        part_copy(k).wait_send()
    for k in range(1, GROUP):
        join_copy(k, False).wait_send()


def local(sizes, mult, trans, up, down, t6, s6, c6, t5, s5, c5, t4, s4, c4):
    n_m, n_s = sizes
    quarter, width = mult.shape
    boxes = quarter * n_s
    slots = GROUP * n_s
    n_ops = trans.shape[0]
    padded = -(-n_ops // STEP) * STEP
    rows = boxes // 8 + PACK
    cap6, cap5, cap4 = t6.shape[2], t5.shape[2], t4.shape[2]
    t6, s6 = jnp.swapaxes(t6, 0, 1), jnp.swapaxes(s6, 0, 1)
    t5, s5, t4, s4 = (jnp.swapaxes(x, 1, 2) for x in (t5, s5, t4, s4))
    index = [pltpu.VMEM(x.shape, x.dtype) for x in (t6, s6, c6, t5, s5, c5, t4, s4, c4)]
    sems = pltpu.SemaphoreType.DMA
    return pl.pallas_call(
        functools.partial(kernel, sizes),
        out_shape=jax.ShapeDtypeStruct((quarter, width), BF16),
        in_specs=[pl.BlockSpec(memory_space=pltpu.HBM)] * 13,
        out_specs=pl.BlockSpec(memory_space=pltpu.VMEM),
        scratch_shapes=[
            pltpu.VMEM((3 * n_s, quarter, width), BF16),
            pltpu.VMEM((GROUP, n_s, PACK, width), BF16),
            pltpu.VMEM((padded, width, width), BF16),
            pltpu.VMEM(up.shape, BF16),
            pltpu.VMEM(down.shape, BF16),
            *index,
            pltpu.VMEM((quarter, width), F32),
            pltpu.VMEM((3 * width, boxes), BF16),
            pltpu.VMEM((width, slots * 8), BF16),
            pltpu.VMEM((width, slots), BF16),
            pltpu.VMEM((padded, cap6), F32),
            pltpu.VMEM((padded, cap6), F32),
            pltpu.VMEM((padded, cap6), F32),
            pltpu.VMEM((padded // 8, 8 * cap5), F32),
            pltpu.VMEM((padded // 8, 8 * cap5), F32),
            pltpu.VMEM((padded // STEP, STEP * cap4), F32),
            pltpu.VMEM((padded // STEP, STEP * cap4), F32),
            pltpu.VMEM((boxes, padded * cap6), BF16),
            pltpu.VMEM((boxes, padded * cap6), BF16),
            pltpu.VMEM((STEP // 2, 2 * width, 2 * cap6), BF16),
            pltpu.VMEM((rows, padded * width), BF16),
            pltpu.VMEM((width, padded * width), BF16),
            pltpu.VMEM((width, padded * cap6), BF16),
            pltpu.VMEM((n_s, quarter + PACK, width), BF16),
            pltpu.VMEM((n_s, quarter + PACK, width), BF16),
            pltpu.VMEM((slots * PACK, slots * 8), BF16),
            pltpu.VMEM((slots * PACK, slots), BF16),
            sems((13,)),
            sems((2 + n_s,)),
            sems((3 * n_s,)),
            sems((2 * n_s,)),
            sems((n_s,)),
            sems((n_s,)),
            sems((GROUP,)),
            sems((GROUP,)),
            sems((n_s,)),
            sems((n_s,)),
        ],
        compiler_params=pltpu.CompilerParams(
            collective_id=0, has_side_effects=True, vmem_limit_bytes=63 * 1024 * 1024
        ),
        name="far_field",
    )(mult, trans, up, down, t6, s6, c6, t5, s5, c5, t4, s4, c4)


def solution(mesh):
    sizes = (mesh.shape["morton"], mesh.shape["sub"])
    placed = (
        P(("morton", "sub"), None),
        P("sub", None, None),
        P(),
        P(),
        P("morton", "sub", None),
        P("morton", "sub", None),
        P("morton", "sub"),
        P("morton", "sub", None),
        P("morton", "sub", None),
        P("morton", "sub"),
        P("morton", "sub", None),
        P("morton", "sub", None),
        P("morton", "sub"),
    )
    return jax.shard_map(
        functools.partial(local, sizes),
        mesh=mesh,
        in_specs=placed,
        out_specs=P(("morton", "sub"), None),
        check_vma=False,
    )
```

```python
import functools

import jax
import jax.numpy as jnp
from jax import lax
from jax.experimental import pallas as pl
from jax.experimental.pallas import tpu as pltpu
from jax.sharding import PartitionSpec as P

BF16 = jnp.bfloat16
F32 = jnp.float32
MESH = pl.DeviceIdType.MESH
GROUP = 8
PACK = 16
STEP = 16


def dot(a, b):
    return jnp.dot(a, b, preferred_element_type=F32)


def dot_nt(a, b):
    return lax.dot_general(a, b, (((1,), (1,)), ((), ())), preferred_element_type=F32)


def column_of(row, height):
    width = row.shape[1]
    at = lax.broadcasted_iota(jnp.int32, (height, width), 0)
    on = lax.broadcasted_iota(jnp.int32, (height, width), 1)
    return jnp.sum(jnp.where(at == on, row, 0.0), axis=1, keepdims=True)


def folded(values, per_row):
    n, cap = values.shape
    lanes = per_row * cap
    j = lax.broadcasted_iota(jnp.int32, (cap, lanes), 0)
    lane = lax.broadcasted_iota(jnp.int32, (cap, lanes), 1)
    spread = jnp.where(lane % cap == j, 1.0, 0.0).astype(BF16)
    wide = dot(values.astype(BF16), spread)
    at = lax.broadcasted_iota(jnp.int32, (n, lanes), 0)
    on = lax.broadcasted_iota(jnp.int32, (n, lanes), 1)
    wide = jnp.where(at % per_row == on // cap, wide, 0.0).astype(BF16)
    out = lax.broadcasted_iota(jnp.int32, (n // per_row, n), 0)
    src = lax.broadcasted_iota(jnp.int32, (n // per_row, n), 1)
    return dot(jnp.where(src // per_row == out, 1.0, 0.0).astype(BF16), wide)


def one_hot(ids, row):
    height, lanes = ids.shape
    rows = jnp.broadcast_to(row, (16, lanes)).astype(BF16)
    same = ids.reshape(height // 16, 16, lanes) == rows[None]
    one, none = jnp.ones((), BF16), jnp.zeros((), BF16)
    return jnp.where(same, one, none).reshape(height, lanes)


def wrapped(value, size):
    return jnp.where(value >= size, value - size, value)


def upward_rows(children, up, wide):
    parents = children.shape[0] // 8
    wide[...] = children.astype(F32)
    rows = [wide[pl.ds(c, parents, stride=8), :] for c in range(8)]
    ops = up.reshape(-1, up.shape[2])
    five = dot(jnp.concatenate(rows, axis=1).astype(BF16), ops).astype(BF16).astype(F32)
    row = jnp.concatenate([five[c : c + 1, :] for c in range(8)], axis=1).astype(BF16)
    pad = jnp.zeros((PACK - parents - 1, five.shape[1]), F32)
    return jnp.concatenate([five, dot(row, ops), pad], axis=0).astype(BF16)


def kernel(
    sizes, mult_hbm, tr_hbm, up_hbm, down_hbm, t6_hbm, s6_hbm, c6_hbm, t5_hbm, s5_hbm, c5_hbm,
    t4_hbm, s4_hbm, c4_hbm, out_ref,
    near, coarse, mats, up, down, t6, s6, c6, t5, s5, c5, t4, s4, c4,
    wide, mt, c5t, c4t, tg6, sr6, bl6, tg5, sr5, tg4, sr4,
    picks, places, apart, gather, turned, products, parts, got, tails,
    got_tails, choose4,
    load, near_send, near_recv, pass_send, pack_send, pack_recv, join_send, join_recv,
    part_send, part_recv, tail_send, tail_recv,
):
    n_m, n_s = sizes
    n_ops, width = tr_hbm.shape[0], tr_hbm.shape[2]
    padded = mats.shape[0]
    quarter = near.shape[1]
    boxes = quarter * n_s
    fives, fours = boxes // 8, boxes // 64
    cap6, cap5, cap4 = t6.shape[2], t5.shape[1], t4.shape[1]
    m, s = lax.axis_index("morton"), lax.axis_index("sub")
    base = m * 0 if n_m == GROUP else m // GROUP * GROUP
    here = m - base
    following = wrapped(m + 1, n_m)
    previous = jnp.where(m == 0, n_m - 1, m - 1)

    barrier = pltpu.get_barrier_semaphore()

    def greet(peer):
        pl.semaphore_signal(barrier, inc=1, device_id=peer, device_id_type=MESH)

    for k in range(1, n_s):
        greet((m, wrapped(s + k, n_s)))
    for k in range(1, GROUP):
        greet((base + wrapped(here + k, GROUP), s))
    expected = n_s - 1 + GROUP - 1
    if n_m > GROUP:
        greet((following, s))
        greet((previous, s))
        expected = expected + 2

    own = near.at[n_s + s]
    pairs = [
        (mult_hbm, own), (up_hbm, up), (c6_hbm, c6), (t6_hbm, t6), (s6_hbm, s6),
        (c5_hbm, c5), (t5_hbm, t5), (s5_hbm, s5), (c4_hbm, c4), (t4_hbm, t4), (s4_hbm, s4),
        (tr_hbm, mats.at[pl.ds(0, n_ops)]), (down_hbm, down),
    ]
    loads = [pltpu.make_async_copy(a, b, load.at[i]) for i, (a, b) in enumerate(pairs)]
    for copy in loads:
        copy.start()

    def remote(src, dst, send, recv, peer):
        return pltpu.make_async_remote_copy(
            src_ref=src, dst_ref=dst, send_sem=send, recv_sem=recv,
            device_id=peer, device_id_type=MESH,
        )

    def halo_copy(side):
        slot = side * 2 * n_s + s
        return remote(
            own, near.at[slot], near_send.at[side], near_recv.at[slot],
            (previous if side else following, s),
        )

    def sub_copy(k, there):
        other = wrapped(s + k, n_s)
        slot = n_s + (other if there else s)
        return remote(
            own, near.at[slot], near_send.at[2 + k], near_recv.at[slot], (m, other)
        )

    def pass_copy(side, k, there):
        other = wrapped(s + k, n_s)
        slot = side * 2 * n_s + (other if there else s)
        return remote(
            near.at[slot], near.at[slot], pass_send.at[side * n_s + k], near_recv.at[slot],
            (m, other),
        )

    def pack_copy(k, there):
        other = wrapped(s + k, n_s)
        slot = coarse.at[here, other if there else s]
        return remote(
            slot, slot, pack_send.at[k], pack_recv.at[other if there else s], (m, other)
        )

    def join_copy(k, there):
        other = wrapped(here + k, GROUP)
        slot = other if there else here
        return remote(
            coarse.at[slot], coarse.at[slot], join_send.at[k], join_recv.at[slot],
            (base + other, s),
        )

    def part_copy(k):
        other = wrapped(s + k, n_s)
        return remote(
            parts.at[other], got.at[k], part_send.at[k], part_recv.at[k], (m, other)
        )

    def tail_copy(k):
        other = wrapped(s + k, n_s)
        return remote(
            tails.at[other], got_tails.at[k], tail_send.at[k], tail_recv.at[k], (m, other)
        )

    loads[0].wait()
    pl.semaphore_wait(barrier, expected)
    for side in range(2):
        halo_copy(side).start()
    for k in range(1, n_s):
        sub_copy(k, False).start()
    loads[1].wait()
    coarse[here, s] = upward_rows(near[n_s + s], up[...], wide)
    for k in range(1, n_s):
        pack_copy(k, False).start()

    for copy in loads[2:11]:
        copy.wait()

    def filled(values, fill):
        if padded == n_ops:
            return values
        more = jnp.full((padded - n_ops, values.shape[1]), fill, F32)
        return jnp.concatenate([values, more], axis=0)

    lane = lax.broadcasted_iota(jnp.int32, (n_ops, cap6), 1).astype(F32)
    live = lane < column_of(c6[...].astype(F32), n_ops)
    tg6[...] = filled(jnp.where(live, t6[:, 0, :].astype(F32), -1.0), -1.0)
    source = s6[:, 0, :]
    block = jnp.where(source >= boxes, 1, 0) + jnp.where(source >= 2 * boxes, 1, 0)
    sr6[...] = filled((source - block * boxes).astype(F32), 0.0)
    bl6[...] = filled(block.astype(F32), 0.0)

    at = lax.broadcasted_iota(jnp.int32, (padded, n_ops), 0)
    on = lax.broadcasted_iota(jnp.int32, (padded, n_ops), 1)
    turn = jnp.where(at == on, 1.0, 0.0).astype(BF16)

    def keys(t_ref, c_ref, per_row, height):
        cap = t_ref.shape[1]
        slot = lax.broadcasted_iota(jnp.int32, (cap, n_ops), 0)
        alive = jnp.where(slot < c_ref[...], t_ref[0] + 1, 0).astype(F32).astype(BF16)
        raw = folded(dot_nt(turn, alive), per_row)
        lane = lax.broadcasted_iota(jnp.int32, raw.shape, 1) // cap
        return jnp.where(raw > 0.0, raw - 1.0 + (lane * height).astype(F32), -1.0)

    def sources(s_ref, per_row):
        return folded(dot_nt(turn, s_ref[0].astype(F32).astype(BF16)), per_row)

    tg5[...] = keys(t5, c5, 8, fives)
    sr5[...] = sources(s5, 8)
    tg4[...] = keys(t4, c4, STEP, PACK)
    sr4[...] = sources(s4, STEP)

    for side in range(2):
        halo_copy(side).wait_recv()
        for k in range(1, n_s):
            pass_copy(side, k, False).start()
    for k in range(1, n_s):
        pack_copy(k, True).wait_recv()
    for k in range(1, GROUP):
        join_copy(k, False).start()
    slots = GROUP * n_s
    p = lax.broadcasted_iota(jnp.int32, (slots, slots * PACK), 0)
    q = lax.broadcasted_iota(jnp.int32, (slots, slots * PACK), 1)
    choose4[...] = jnp.where(q == p * PACK + 8, 1.0, 0.0).astype(BF16)

    apart[...] = jnp.zeros(apart.shape, BF16)
    for o in range(n_ops, padded):
        mats[o] = jnp.zeros(mats.shape[1:], BF16)
    ids = lax.broadcasted_iota(jnp.int32, (boxes, cap6), 0).astype(F32).astype(BF16)

    @pl.loop(0, padded // STEP)
    def _(step):
        for j in range(STEP):
            lanes = pl.ds(pl.multiple_of(step * STEP * cap6 + j * cap6, cap6), cap6)
            picks[:, lanes] = one_hot(ids, sr6[pl.ds(step * STEP + j, 1), :])

    r = lax.broadcasted_iota(jnp.int32, (width, width), 0)
    c = lax.broadcasted_iota(jnp.int32, (width, width), 1)
    eye = jnp.where(r == c, 1.0, 0.0).astype(BF16)

    loads[11].wait()

    @pl.loop(0, padded // STEP)
    def _(step):
        for pair in range(STEP // 2):
            both = mats[pl.ds(step * STEP + 2 * pair, 2)].reshape(2 * width, width)
            start = step * STEP * width + 2 * pair * width
            lanes = pl.ds(pl.multiple_of(start, 2 * width), 2 * width)
            turned[:, lanes] = dot_nt(eye, both).astype(BF16)

    for k in range(1, n_s):
        sub_copy(k, True).wait_recv()
    for side in range(2):
        for k in range(1, n_s):
            pass_copy(side, k, True).wait_recv()

    nearby = near[...].reshape(3, boxes, width)
    for block in range(3):
        rows = dot_nt(eye, nearby[block])
        if block == 0:
            rows = jnp.where(m == 0, 0.0, rows)
        if block == 2:
            rows = jnp.where(m == n_m - 1, 0.0, rows)
        mt[pl.ds(block * width, width), :] = rows.astype(BF16)

    for k in range(1, GROUP):
        join_copy(k, True).wait_recv()
    message = coarse[...].reshape(slots, PACK, width)
    rows5 = message.astype(F32)[:, :8, :].reshape(slots * 8, width).astype(BF16)
    c5t[...] = dot_nt(eye, rows5).astype(BF16)
    rows4 = dot(choose4[...], message.reshape(slots * PACK, width)).astype(BF16)
    c4t[...] = dot_nt(eye, rows4).astype(BF16)

    def numbers(height, lanes):
        return lax.broadcasted_iota(jnp.int32, (height, lanes), 0).astype(F32).astype(BF16)

    source5, target5 = numbers(slots * 8, 8 * cap5), numbers(8 * fives, 8 * cap5)
    source4, target4 = numbers(slots, STEP * cap4), numbers(STEP * PACK, STEP * cap4)

    for step in range(padded // STEP):

        def at(o, step=step):
            return pl.ds((step * STEP + o) * width, width)

        for half in range(STEP // 8):
            row = step * (STEP // 8) + half
            found = dot(c5t[...], one_hot(source5, sr5[pl.ds(row, 1), :])).astype(BF16)
            placed = dot_nt(one_hot(target5, tg5[pl.ds(row, 1), :]), found).astype(BF16)
            for o in range(8):
                gather[pl.ds(0, fives), at(half * 8 + o)] = placed[o * fives : (o + 1) * fives]
        found = dot(c4t[...], one_hot(source4, sr4[pl.ds(step, 1), :])).astype(BF16)
        placed = dot_nt(one_hot(target4, tg4[pl.ds(step, 1), :]), found).astype(BF16)
        for o in range(STEP):
            gather[pl.ds(fives, PACK), at(o)] = placed[o * PACK : (o + 1) * PACK]

    low = 0.0
    for step in range(padded // STEP):
        ops = mats[pl.ds(step * STEP, STEP)].reshape(STEP * width, width)
        low = low + dot(gather[:, pl.ds(step * STEP * width, STEP * width)], ops)

    six, five, four = boxes // n_s, fives // n_s, fours // n_s
    for part in range(n_s):
        last = fives + part * four
        tail = jnp.concatenate(
            [
                low[part * five : (part + 1) * five] * 0.5,
                low[last : last + four] * 0.25,
                jnp.zeros((PACK - five - four, width), F32),
            ],
            axis=0,
        )
        tails[part] = tail.astype(BF16)
    for k in range(1, n_s):
        tail_copy(k).start()

    quads = STEP // 4

    @pl.loop(0, padded // STEP)
    def _(step):
        def pick(quad):
            start = step * STEP * cap6 + 4 * quad * cap6
            lanes = pl.ds(pl.multiple_of(start, 4 * cap6), 4 * cap6)
            found = dot(mt[...], picks[:, lanes]).astype(BF16)
            for k in range(4):
                o = 4 * quad + k
                head = bl6[pl.ds(step * STEP + o, 1), :]
                head = jnp.broadcast_to(head, (16, cap6)).astype(BF16)[None]
                piece = found[:, k * cap6 : (k + 1) * cap6].reshape(3, width // 16, 16, cap6)
                chosen = jnp.where(head == 1.0, piece[1], piece[2])
                chosen = jnp.where(head == 0.0, piece[0], chosen)
                half = o % 2
                apart[o // 2, pl.ds(half * width, width), pl.ds(half * cap6, cap6)] = (
                    chosen.reshape(width, cap6)
                )
                lanes = pl.ds(pl.multiple_of((step * STEP + o) * cap6, cap6), cap6)
                places[:, lanes] = one_hot(ids, tg6[pl.ds(step * STEP + o, 1), :])

        def translate(pair):
            start = step * STEP * width + 2 * pair * width
            lanes = pl.ds(pl.multiple_of(start, 2 * width), 2 * width)
            start = step * STEP * cap6 + 2 * pair * cap6
            slots = pl.ds(pl.multiple_of(start, 2 * cap6), 2 * cap6)
            products[:, slots] = dot(turned[:, lanes], apart[pair]).astype(BF16)

        for turn in range(quads + 1):
            if turn >= 1:
                translate(2 * turn - 2)
                translate(2 * turn - 1)
            if turn < quads:
                pick(turn)

    total = 0.0
    for step in range(padded // STEP):
        lanes = pl.ds(step * STEP * cap6, STEP * cap6)
        total = total + dot_nt(products[:, lanes], places[:, lanes])
    total = total.T
    for part in range(n_s):
        parts[part] = total[part * six : (part + 1) * six].astype(BF16)
    for k in range(1, n_s):
        part_copy(k).start()
    loads[12].wait()
    below = tails[s].astype(F32)
    for k in range(1, n_s):
        tail_copy(k).wait_recv()
        below = below + got_tails[k].astype(F32)
    row = below[five : five + 1, :].astype(BF16)
    spread = [dot(row, down[c]) for c in range(8)]
    mid = (below[:five, :] + jnp.concatenate(spread, axis=0)).astype(BF16)
    for c in range(8):
        wide[pl.ds(c, six // 8, stride=8), :] = dot(mid, down[c])
    whole = parts[s].astype(F32)
    for k in range(1, n_s):
        part_copy(k).wait_recv()
        whole = whole + got[k].astype(F32)
    out_ref[...] = (wide[...] + whole).astype(BF16)

    for side in range(2):
        halo_copy(side).wait_send()
        for k in range(1, n_s):
            pass_copy(side, k, False).wait_send()
    for k in range(1, n_s):
        sub_copy(k, False).wait_send()
        pack_copy(k, False).wait_send()
        part_copy(k).wait_send()
        tail_copy(k).wait_send()
    for k in range(1, GROUP):
        join_copy(k, False).wait_send()


def local(sizes, mult, trans, up, down, t6, s6, c6, t5, s5, c5, t4, s4, c4):
    n_m, n_s = sizes
    quarter, width = mult.shape
    boxes = quarter * n_s
    slots = GROUP * n_s
    n_ops = trans.shape[0]
    padded = -(-n_ops // STEP) * STEP
    rows = boxes // 8 + PACK
    cap6, cap5, cap4 = t6.shape[2], t5.shape[2], t4.shape[2]
    t6, s6 = jnp.swapaxes(t6, 0, 1), jnp.swapaxes(s6, 0, 1)
    t5, s5, t4, s4 = (jnp.swapaxes(x, 1, 2) for x in (t5, s5, t4, s4))
    index = [pltpu.VMEM(x.shape, x.dtype) for x in (t6, s6, c6, t5, s5, c5, t4, s4, c4)]
    sems = pltpu.SemaphoreType.DMA
    return pl.pallas_call(
        functools.partial(kernel, sizes),
        out_shape=jax.ShapeDtypeStruct((quarter, width), BF16),
        in_specs=[pl.BlockSpec(memory_space=pltpu.HBM)] * 13,
        out_specs=pl.BlockSpec(memory_space=pltpu.VMEM),
        scratch_shapes=[
            pltpu.VMEM((3 * n_s, quarter, width), BF16),
            pltpu.VMEM((GROUP, n_s, PACK, width), BF16),
            pltpu.VMEM((padded, width, width), BF16),
            pltpu.VMEM(up.shape, BF16),
            pltpu.VMEM(down.shape, BF16),
            *index,
            pltpu.VMEM((quarter, width), F32),
            pltpu.VMEM((3 * width, boxes), BF16),
            pltpu.VMEM((width, slots * 8), BF16),
            pltpu.VMEM((width, slots), BF16),
            pltpu.VMEM((padded, cap6), F32),
            pltpu.VMEM((padded, cap6), F32),
            pltpu.VMEM((padded, cap6), F32),
            pltpu.VMEM((padded // 8, 8 * cap5), F32),
            pltpu.VMEM((padded // 8, 8 * cap5), F32),
            pltpu.VMEM((padded // STEP, STEP * cap4), F32),
            pltpu.VMEM((padded // STEP, STEP * cap4), F32),
            pltpu.VMEM((boxes, padded * cap6), BF16),
            pltpu.VMEM((boxes, padded * cap6), BF16),
            pltpu.VMEM((STEP // 2, 2 * width, 2 * cap6), BF16),
            pltpu.VMEM((rows, padded * width), BF16),
            pltpu.VMEM((width, padded * width), BF16),
            pltpu.VMEM((width, padded * cap6), BF16),
            pltpu.VMEM((n_s, quarter, width), BF16),
            pltpu.VMEM((n_s, quarter, width), BF16),
            pltpu.VMEM((n_s, PACK, width), BF16),
            pltpu.VMEM((n_s, PACK, width), BF16),
            pltpu.VMEM((slots, slots * PACK), BF16),
            sems((13,)),
            sems((2 + n_s,)),
            sems((3 * n_s,)),
            sems((2 * n_s,)),
            sems((n_s,)),
            sems((n_s,)),
            sems((GROUP,)),
            sems((GROUP,)),
            sems((n_s,)),
            sems((n_s,)),
            sems((n_s,)),
            sems((n_s,)),
        ],
        compiler_params=pltpu.CompilerParams(
            collective_id=0, has_side_effects=True, vmem_limit_bytes=63 * 1024 * 1024
        ),
        name="far_field",
    )(mult, trans, up, down, t6, s6, c6, t5, s5, c5, t4, s4, c4)


def solution(mesh):
    sizes = (mesh.shape["morton"], mesh.shape["sub"])
    placed = (
        P(("morton", "sub"), None),
        P("sub", None, None),
        P(),
        P(),
        P("morton", "sub", None),
        P("morton", "sub", None),
        P("morton", "sub"),
        P("morton", "sub", None),
        P("morton", "sub", None),
        P("morton", "sub"),
        P("morton", "sub", None),
        P("morton", "sub", None),
        P("morton", "sub"),
    )
    return jax.shard_map(
        functools.partial(local, sizes),
        mesh=mesh,
        in_specs=placed,
        out_specs=P(("morton", "sub"), None),
        check_vma=False,
    )
```

```python
import functools

import jax
import jax.numpy as jnp
from jax import lax
from jax.experimental import pallas as pl
from jax.experimental.pallas import tpu as pltpu
from jax.sharding import PartitionSpec as P

BF16 = jnp.bfloat16
F32 = jnp.float32
MESH = pl.DeviceIdType.MESH
GROUP = 8
PACK = 16
STEP = 16


def dot(a, b):
    return jnp.dot(a, b, preferred_element_type=F32)


def dot_nt(a, b):
    return lax.dot_general(a, b, (((1,), (1,)), ((), ())), preferred_element_type=F32)


def column_of(row, height):
    width = row.shape[1]
    at = lax.broadcasted_iota(jnp.int32, (height, width), 0)
    on = lax.broadcasted_iota(jnp.int32, (height, width), 1)
    return jnp.sum(jnp.where(at == on, row, 0.0), axis=1, keepdims=True)


def folded(values, per_row):
    n, cap = values.shape
    lanes = per_row * cap
    j = lax.broadcasted_iota(jnp.int32, (cap, lanes), 0)
    lane = lax.broadcasted_iota(jnp.int32, (cap, lanes), 1)
    spread = jnp.where(lane % cap == j, 1.0, 0.0).astype(BF16)
    wide = dot(values.astype(BF16), spread)
    at = lax.broadcasted_iota(jnp.int32, (n, lanes), 0)
    on = lax.broadcasted_iota(jnp.int32, (n, lanes), 1)
    wide = jnp.where(at % per_row == on // cap, wide, 0.0).astype(BF16)
    out = lax.broadcasted_iota(jnp.int32, (n // per_row, n), 0)
    src = lax.broadcasted_iota(jnp.int32, (n // per_row, n), 1)
    return dot(jnp.where(src // per_row == out, 1.0, 0.0).astype(BF16), wide)


def one_hot(ids, row):
    height, lanes = ids.shape
    rows = jnp.broadcast_to(row, (16, lanes)).astype(BF16)
    same = ids.reshape(height // 16, 16, lanes) == rows[None]
    one, none = jnp.ones((), BF16), jnp.zeros((), BF16)
    return jnp.where(same, one, none).reshape(height, lanes)


def wrapped(value, size):
    return jnp.where(value >= size, value - size, value)


def upward_rows(children, up, wide):
    parents = children.shape[0] // 8
    wide[...] = children.astype(F32)
    rows = [wide[pl.ds(c, parents, stride=8), :] for c in range(8)]
    ops = up.reshape(-1, up.shape[2])
    five = dot(jnp.concatenate(rows, axis=1).astype(BF16), ops).astype(BF16).astype(F32)
    row = jnp.concatenate([five[c : c + 1, :] for c in range(8)], axis=1).astype(BF16)
    pad = jnp.zeros((PACK - parents - 1, five.shape[1]), F32)
    return jnp.concatenate([five, dot(row, ops), pad], axis=0).astype(BF16)


def kernel(
    sizes, mult_hbm, tr_hbm, up_hbm, down_hbm, t6_hbm, s6_hbm, c6_hbm, t5_hbm, s5_hbm, c5_hbm,
    t4_hbm, s4_hbm, c4_hbm, out_ref,
    near, coarse, mats, up, down, t6, s6, c6, t5, s5, c5, t4, s4, c4,
    wide, mt, c5t, c4t, tg6, sr6, bl6, tg5, sr5, tg4, sr4,
    picks, places, apart, gather, turned, products, parts, got, choose5,
    choose4,
    load, near_send, near_recv, pass_send, pack_send, pack_recv, join_send, join_recv,
    part_send, part_recv,
):
    n_m, n_s = sizes
    n_ops, width = tr_hbm.shape[0], tr_hbm.shape[2]
    padded = mats.shape[0]
    quarter = near.shape[1]
    boxes = quarter * n_s
    fives, fours = boxes // 8, boxes // 64
    cap6, cap5, cap4 = t6.shape[2], t5.shape[1], t4.shape[1]
    m, s = lax.axis_index("morton"), lax.axis_index("sub")
    base = m * 0 if n_m == GROUP else m // GROUP * GROUP
    here = m - base
    following = wrapped(m + 1, n_m)
    previous = jnp.where(m == 0, n_m - 1, m - 1)

    barrier = pltpu.get_barrier_semaphore()

    def greet(peer):
        pl.semaphore_signal(barrier, inc=1, device_id=peer, device_id_type=MESH)

    for k in range(1, n_s):
        greet((m, wrapped(s + k, n_s)))
    for k in range(1, GROUP):
        greet((base + wrapped(here + k, GROUP), s))
    expected = n_s - 1 + GROUP - 1
    if n_m > GROUP:
        greet((following, s))
        greet((previous, s))
        expected = expected + 2

    own = near.at[n_s + s]
    pairs = [
        (mult_hbm, own), (up_hbm, up), (c6_hbm, c6), (t6_hbm, t6), (s6_hbm, s6),
        (c5_hbm, c5), (t5_hbm, t5), (s5_hbm, s5), (c4_hbm, c4), (t4_hbm, t4), (s4_hbm, s4),
        (tr_hbm, mats.at[pl.ds(0, n_ops)]), (down_hbm, down),
    ]
    loads = [pltpu.make_async_copy(a, b, load.at[i]) for i, (a, b) in enumerate(pairs)]
    for copy in loads:
        copy.start()

    def remote(src, dst, send, recv, peer):
        return pltpu.make_async_remote_copy(
            src_ref=src, dst_ref=dst, send_sem=send, recv_sem=recv,
            device_id=peer, device_id_type=MESH,
        )

    def halo_copy(side):
        slot = side * 2 * n_s + s
        return remote(
            own, near.at[slot], near_send.at[side], near_recv.at[slot],
            (previous if side else following, s),
        )

    def sub_copy(k, there):
        other = wrapped(s + k, n_s)
        slot = n_s + (other if there else s)
        return remote(
            own, near.at[slot], near_send.at[2 + k], near_recv.at[slot], (m, other)
        )

    def pass_copy(side, k, there):
        other = wrapped(s + k, n_s)
        slot = side * 2 * n_s + (other if there else s)
        return remote(
            near.at[slot], near.at[slot], pass_send.at[side * n_s + k], near_recv.at[slot],
            (m, other),
        )

    def pack_copy(k, there):
        other = wrapped(s + k, n_s)
        slot = coarse.at[here, other if there else s]
        return remote(
            slot, slot, pack_send.at[k], pack_recv.at[other if there else s], (m, other)
        )

    def join_copy(k, there):
        other = wrapped(here + k, GROUP)
        slot = other if there else here
        return remote(
            coarse.at[slot], coarse.at[slot], join_send.at[k], join_recv.at[slot],
            (base + other, s),
        )

    def part_copy(k):
        other = wrapped(s + k, n_s)
        return remote(
            parts.at[other], got.at[k], part_send.at[k], part_recv.at[k], (m, other)
        )

    for copy in loads[2:11]:
        copy.wait()

    def filled(values, fill):
        if padded == n_ops:
            return values
        more = jnp.full((padded - n_ops, values.shape[1]), fill, F32)
        return jnp.concatenate([values, more], axis=0)

    lane = lax.broadcasted_iota(jnp.int32, (n_ops, cap6), 1).astype(F32)
    live = lane < column_of(c6[...].astype(F32), n_ops)
    tg6[...] = filled(jnp.where(live, t6[:, 0, :].astype(F32), -1.0), -1.0)
    source = s6[:, 0, :]
    block = jnp.where(source >= boxes, 1, 0) + jnp.where(source >= 2 * boxes, 1, 0)
    sr6[...] = filled((source - block * boxes).astype(F32), 0.0)
    bl6[...] = filled(block.astype(F32), 0.0)

    at = lax.broadcasted_iota(jnp.int32, (padded, n_ops), 0)
    on = lax.broadcasted_iota(jnp.int32, (padded, n_ops), 1)
    turn = jnp.where(at == on, 1.0, 0.0).astype(BF16)

    def keys(t_ref, c_ref, per_row, height):
        cap = t_ref.shape[1]
        slot = lax.broadcasted_iota(jnp.int32, (cap, n_ops), 0)
        alive = jnp.where(slot < c_ref[...], t_ref[0] + 1, 0).astype(F32).astype(BF16)
        raw = folded(dot_nt(turn, alive), per_row)
        lane = lax.broadcasted_iota(jnp.int32, raw.shape, 1) // cap
        return jnp.where(raw > 0.0, raw - 1.0 + (lane * height).astype(F32), -1.0)

    def sources(s_ref, per_row):
        return folded(dot_nt(turn, s_ref[0].astype(F32).astype(BF16)), per_row)

    tg5[...] = keys(t5, c5, 8, fives)
    sr5[...] = sources(s5, 8)
    tg4[...] = keys(t4, c4, STEP, PACK)
    sr4[...] = sources(s4, STEP)

    loads[0].wait()
    pl.semaphore_wait(barrier, expected)
    for side in range(2):
        halo_copy(side).start()
    for k in range(1, n_s):
        sub_copy(k, False).start()
    loads[1].wait()
    coarse[here, s] = upward_rows(near[n_s + s], up[...], wide)
    for k in range(1, n_s):
        pack_copy(k, False).start()

    apart[...] = jnp.zeros(apart.shape, BF16)
    for o in range(n_ops, padded):
        mats[o] = jnp.zeros(mats.shape[1:], BF16)
    ids = lax.broadcasted_iota(jnp.int32, (boxes, cap6), 0).astype(F32).astype(BF16)

    @pl.loop(0, padded // STEP)
    def _(step):
        for j in range(STEP):
            lanes = pl.ds(pl.multiple_of(step * STEP * cap6 + j * cap6, cap6), cap6)
            picks[:, lanes] = one_hot(ids, sr6[pl.ds(step * STEP + j, 1), :])

    for side in range(2):
        halo_copy(side).wait_recv()
        for k in range(1, n_s):
            pass_copy(side, k, False).start()
    for k in range(1, n_s):
        pack_copy(k, True).wait_recv()
    for k in range(1, GROUP):
        join_copy(k, False).start()
    slots = GROUP * n_s
    q = lax.broadcasted_iota(jnp.int32, (slots * PACK, slots * 8), 0)
    p = lax.broadcasted_iota(jnp.int32, (slots * PACK, slots * 8), 1)
    choose5[...] = jnp.where(q == p // 8 * PACK + p % 8, 1.0, 0.0).astype(BF16)
    q = lax.broadcasted_iota(jnp.int32, (slots * PACK, slots), 0)
    p = lax.broadcasted_iota(jnp.int32, (slots * PACK, slots), 1)
    choose4[...] = jnp.where(q == p * PACK + 8, 1.0, 0.0).astype(BF16)

    r = lax.broadcasted_iota(jnp.int32, (width, width), 0)
    c = lax.broadcasted_iota(jnp.int32, (width, width), 1)
    eye = jnp.where(r == c, 1.0, 0.0).astype(BF16)

    loads[11].wait()

    @pl.loop(0, padded // STEP)
    def _(step):
        for pair in range(STEP // 2):
            both = mats[pl.ds(step * STEP + 2 * pair, 2)].reshape(2 * width, width)
            start = step * STEP * width + 2 * pair * width
            lanes = pl.ds(pl.multiple_of(start, 2 * width), 2 * width)
            turned[:, lanes] = dot_nt(eye, both).astype(BF16)

    for k in range(1, n_s):
        sub_copy(k, True).wait_recv()
    for side in range(2):
        for k in range(1, n_s):
            pass_copy(side, k, True).wait_recv()

    nearby = near[...].reshape(3, boxes, width)
    for block in range(3):
        rows = dot_nt(eye, nearby[block])
        if block == 0:
            rows = jnp.where(m == 0, 0.0, rows)
        if block == 2:
            rows = jnp.where(m == n_m - 1, 0.0, rows)
        mt[pl.ds(block * width, width), :] = rows.astype(BF16)

    quads = STEP // 4

    @pl.loop(0, padded // STEP)
    def _(step):
        def pick(quad):
            start = step * STEP * cap6 + 4 * quad * cap6
            lanes = pl.ds(pl.multiple_of(start, 4 * cap6), 4 * cap6)
            found = dot(mt[...], picks[:, lanes]).astype(BF16)
            for k in range(4):
                o = 4 * quad + k
                head = bl6[pl.ds(step * STEP + o, 1), :]
                head = jnp.broadcast_to(head, (16, cap6)).astype(BF16)[None]
                piece = found[:, k * cap6 : (k + 1) * cap6].reshape(3, width // 16, 16, cap6)
                chosen = jnp.where(head == 1.0, piece[1], piece[2])
                chosen = jnp.where(head == 0.0, piece[0], chosen)
                half = o % 2
                apart[o // 2, pl.ds(half * width, width), pl.ds(half * cap6, cap6)] = (
                    chosen.reshape(width, cap6)
                )
                lanes = pl.ds(pl.multiple_of((step * STEP + o) * cap6, cap6), cap6)
                places[:, lanes] = one_hot(ids, tg6[pl.ds(step * STEP + o, 1), :])

        def translate(pair):
            start = step * STEP * width + 2 * pair * width
            lanes = pl.ds(pl.multiple_of(start, 2 * width), 2 * width)
            start = step * STEP * cap6 + 2 * pair * cap6
            slots = pl.ds(pl.multiple_of(start, 2 * cap6), 2 * cap6)
            products[:, slots] = dot(turned[:, lanes], apart[pair]).astype(BF16)

        for turn in range(quads + 1):
            if turn >= 1:
                translate(2 * turn - 2)
                translate(2 * turn - 1)
            if turn < quads:
                pick(turn)

    for k in range(1, GROUP):
        join_copy(k, True).wait_recv()
    packed = dot_nt(eye, coarse[...].reshape(slots * PACK, width)).astype(BF16)
    c5t[...] = dot(packed, choose5[...]).astype(BF16)
    c4t[...] = dot(packed, choose4[...]).astype(BF16)

    def numbers(height, lanes):
        return lax.broadcasted_iota(jnp.int32, (height, lanes), 0).astype(F32).astype(BF16)

    source5, target5 = numbers(slots * 8, 8 * cap5), numbers(8 * fives, 8 * cap5)
    source4, target4 = numbers(slots, STEP * cap4), numbers(STEP * PACK, STEP * cap4)

    for step in range(padded // STEP):

        def at(o, step=step):
            return pl.ds((step * STEP + o) * width, width)

        for half in range(STEP // 8):
            row = step * (STEP // 8) + half
            found = dot(c5t[...], one_hot(source5, sr5[pl.ds(row, 1), :])).astype(BF16)
            placed = dot_nt(one_hot(target5, tg5[pl.ds(row, 1), :]), found).astype(BF16)
            for o in range(8):
                gather[pl.ds(0, fives), at(half * 8 + o)] = placed[o * fives : (o + 1) * fives]
        found = dot(c4t[...], one_hot(source4, sr4[pl.ds(step, 1), :])).astype(BF16)
        placed = dot_nt(one_hot(target4, tg4[pl.ds(step, 1), :]), found).astype(BF16)
        for o in range(STEP):
            gather[pl.ds(fives, PACK), at(o)] = placed[o * PACK : (o + 1) * PACK]

    total, low = 0.0, 0.0
    for step in range(padded // STEP):
        lanes = pl.ds(step * STEP * cap6, STEP * cap6)
        total = total + dot_nt(products[:, lanes], places[:, lanes])
        ops = mats[pl.ds(step * STEP, STEP)].reshape(STEP * width, width)
        low = low + dot(gather[:, pl.ds(step * STEP * width, STEP * width)], ops)
    total = total.T

    six, five, four = boxes // n_s, fives // n_s, fours // n_s
    for part in range(n_s):
        parts[part, pl.ds(0, six), :] = total[part * six : (part + 1) * six].astype(BF16)
        last = fives + part * four
        tail = jnp.concatenate(
            [
                low[part * five : (part + 1) * five] * 0.5,
                low[last : last + four] * 0.25,
                jnp.zeros((PACK - five - four, width), F32),
            ],
            axis=0,
        )
        parts[part, pl.ds(six, PACK), :] = tail.astype(BF16)
    for k in range(1, n_s):
        part_copy(k).start()
    loads[12].wait()
    whole = parts[s].astype(F32)
    for k in range(1, n_s):
        part_copy(k).wait_recv()
        whole = whole + got[k].astype(F32)
    row = whole[six + five : six + five + 1, :].astype(BF16)
    spread = [dot(row, down[c]) for c in range(8)]
    mid = (whole[six : six + five, :] + jnp.concatenate(spread, axis=0)).astype(BF16)
    for c in range(8):
        wide[pl.ds(c, six // 8, stride=8), :] = dot(mid, down[c])
    out_ref[...] = (wide[...] + whole[:six, :]).astype(BF16)

    for side in range(2):
        halo_copy(side).wait_send()
        for k in range(1, n_s):
            pass_copy(side, k, False).wait_send()
    for k in range(1, n_s):
        sub_copy(k, False).wait_send()
        pack_copy(k, False).wait_send()
        part_copy(k).wait_send()
    for k in range(1, GROUP):
        join_copy(k, False).wait_send()


def local(sizes, mult, trans, up, down, t6, s6, c6, t5, s5, c5, t4, s4, c4):
    n_m, n_s = sizes
    quarter, width = mult.shape
    boxes = quarter * n_s
    slots = GROUP * n_s
    n_ops = trans.shape[0]
    padded = -(-n_ops // STEP) * STEP
    rows = boxes // 8 + PACK
    cap6, cap5, cap4 = t6.shape[2], t5.shape[2], t4.shape[2]
    t6, s6 = jnp.swapaxes(t6, 0, 1), jnp.swapaxes(s6, 0, 1)
    t5, s5, t4, s4 = (jnp.swapaxes(x, 1, 2) for x in (t5, s5, t4, s4))
    index = [pltpu.VMEM(x.shape, x.dtype) for x in (t6, s6, c6, t5, s5, c5, t4, s4, c4)]
    sems = pltpu.SemaphoreType.DMA
    return pl.pallas_call(
        functools.partial(kernel, sizes),
        out_shape=jax.ShapeDtypeStruct((quarter, width), BF16),
        in_specs=[pl.BlockSpec(memory_space=pltpu.HBM)] * 13,
        out_specs=pl.BlockSpec(memory_space=pltpu.VMEM),
        scratch_shapes=[
            pltpu.VMEM((3 * n_s, quarter, width), BF16),
            pltpu.VMEM((GROUP, n_s, PACK, width), BF16),
            pltpu.VMEM((padded, width, width), BF16),
            pltpu.VMEM(up.shape, BF16),
            pltpu.VMEM(down.shape, BF16),
            *index,
            pltpu.VMEM((quarter, width), F32),
            pltpu.VMEM((3 * width, boxes), BF16),
            pltpu.VMEM((width, slots * 8), BF16),
            pltpu.VMEM((width, slots), BF16),
            pltpu.VMEM((padded, cap6), F32),
            pltpu.VMEM((padded, cap6), F32),
            pltpu.VMEM((padded, cap6), F32),
            pltpu.VMEM((padded // 8, 8 * cap5), F32),
            pltpu.VMEM((padded // 8, 8 * cap5), F32),
            pltpu.VMEM((padded // STEP, STEP * cap4), F32),
            pltpu.VMEM((padded // STEP, STEP * cap4), F32),
            pltpu.VMEM((boxes, padded * cap6), BF16),
            pltpu.VMEM((boxes, padded * cap6), BF16),
            pltpu.VMEM((STEP // 2, 2 * width, 2 * cap6), BF16),
            pltpu.VMEM((rows, padded * width), BF16),
            pltpu.VMEM((width, padded * width), BF16),
            pltpu.VMEM((width, padded * cap6), BF16),
            pltpu.VMEM((n_s, quarter + PACK, width), BF16),
            pltpu.VMEM((n_s, quarter + PACK, width), BF16),
            pltpu.VMEM((slots * PACK, slots * 8), BF16),
            pltpu.VMEM((slots * PACK, slots), BF16),
            sems((13,)),
            sems((2 + n_s,)),
            sems((3 * n_s,)),
            sems((2 * n_s,)),
            sems((n_s,)),
            sems((n_s,)),
            sems((GROUP,)),
            sems((GROUP,)),
            sems((n_s,)),
            sems((n_s,)),
        ],
        compiler_params=pltpu.CompilerParams(
            collective_id=0, has_side_effects=True, vmem_limit_bytes=63 * 1024 * 1024
        ),
        name="far_field",
    )(mult, trans, up, down, t6, s6, c6, t5, s5, c5, t4, s4, c4)


def solution(mesh):
    sizes = (mesh.shape["morton"], mesh.shape["sub"])
    placed = (
        P(("morton", "sub"), None),
        P("sub", None, None),
        P(),
        P(),
        P("morton", "sub", None),
        P("morton", "sub", None),
        P("morton", "sub"),
        P("morton", "sub", None),
        P("morton", "sub", None),
        P("morton", "sub"),
        P("morton", "sub", None),
        P("morton", "sub", None),
        P("morton", "sub"),
    )
    return jax.shard_map(
        functools.partial(local, sizes),
        mesh=mesh,
        in_specs=placed,
        out_specs=P(("morton", "sub"), None),
        check_vma=False,
    )
```
